128 devices in a mesh: dp: 8 (over x, core), blk: 16 (over y, z).
Axes of the slice: x: 4, y: 4, z: 4, core: 2. Of those that a mesh axis runs over, the one named last changes fastest.
Arguments:
- embedding: bfloat16 [512, 256, 1024], P(('dp', 'blk')), may hold values from -6 to 6
- subspace: float32 [512, 256, 64], P(('dp', 'blk')), may hold values from -6 to 6
- degree: float32 [512, 256], P(('dp', 'blk')), may hold values from 300 to 3000
- neighbours: int32 [512, 16], P(('dp', 'blk')), may hold values from 0 to 63, as said below
- counts: int32 [512], P(('dp', 'blk')), may hold values from 1 to 16, as said below
Outputs:
- basis_next: float32 [512, 256, 64], P(('dp', 'blk'))
The draws below stay inside these ranges and needn't reach their ends.
Inputs may be any that keep to these rules, and one draw needn't show every extreme that they name: `neighbours`: block g's slots name blocks of its own group by index inside the group, never g itself; the used slots of a block name distinct blocks; slots from counts[g] on are unused. `counts`: some block uses all 16 slots in every draw.
All inputs are finite; a program needn't handle non-finite values.
Results may differ from the reference program's by a relative error of at most 0.0042.
Values may be sent and summed in bfloat16 or wider, within the bound.
No kernel may reach another device: no remote copies, remote signals or barrier semaphores. Data moves between devices by JAX's collectives and lax.ppermute only.
A program may use at most 128 MiB of HBM per device.

```python
import math
import jax
import jax.numpy as jnp
from jax import lax

E = 1024
K = 64
R = 256
CAP = 16
BLK_DEV = 4
GROUP = 64
BLOCKS = 512
N_BLK = 16


topic_total = 8


def draw_embedding(key, part):
    key = jax.random.fold_in(key, 5)
    shared_key, center_key, assign_key, jitter_key = jax.random.split(key, 4)
    topic = jax.random.randint(assign_key, (BLOCKS, R), 0, topic_total, dtype=jnp.int32)
    common = 0.5 * jax.random.normal(shared_key, (E,), jnp.float32)
    centers = 0.5 * jax.random.normal(center_key, (topic_total, E), jnp.float32)
    jitter = 1.2247 * jax.random.normal(jitter_key, (BLOCKS, R, E), jnp.float32)
    values = common[None, None, :] + jnp.take(centers, topic, axis=0) + jitter
    return jnp.clip(values, -6.0, 6.0).astype(jnp.bfloat16)


def draw_neighbours(key, part):
    key = jax.random.fold_in(key, 11)
    within = jnp.arange(BLOCKS, dtype=jnp.int32) % GROUP
    candidates = jnp.arange(GROUP - 1, dtype=jnp.int32)
    scores = jax.random.randint(key, (BLOCKS, GROUP - 1), 0, 32768, dtype=jnp.int32)
    scores = scores * GROUP + candidates[None, :]
    order = jnp.argsort(scores, axis=1, stable=True).astype(jnp.int32)
    jumps = order[:, :CAP] + 1
    return ((within[:, None] + jumps) % GROUP).astype(jnp.int32)


def draw_counts(key, part):
    key = jax.random.fold_in(key, 23)
    base_key, heavy_key, pick_key = jax.random.split(key, 3)
    device_total = BLOCKS // BLK_DEV
    base = jax.random.randint(base_key, (BLOCKS,), 1, CAP // 4 + 1, dtype=jnp.int32)
    heavy = jax.random.randint(heavy_key, (device_total,), 0, 8, dtype=jnp.int32) == 0
    chosen = jax.random.randint(pick_key, (), 0, device_total, dtype=jnp.int32)
    heavy = heavy | (jnp.arange(device_total, dtype=jnp.int32) == chosen)
    owner = jnp.arange(BLOCKS, dtype=jnp.int32) // BLK_DEV
    return jnp.where(heavy[owner], CAP, base).astype(jnp.int32)


def block_scale(key, shape, cuts, smallest, largest):
    level, own = 1.0, jax.random.fold_in(key, 6)
    for position, blocks in cuts:
        draws = jnp.exp(jax.random.uniform(jax.random.fold_in(own, position), (blocks,), jnp.float32, smallest / len(cuts), largest / len(cuts)))
        level = level * jnp.repeat(draws, shape[position] // blocks).reshape([-1 if axis == position else 1 for axis in range(len(shape))])
    return level


def bell_draw(own_key, extent, deviation, limit, cuts=(), kind=jnp.bfloat16):
    result = deviation * jax.random.normal(own_key, extent, jnp.float32)
    if cuts:
        result = result * block_scale(own_key, extent, cuts, -0.22, 0.18)
    return jnp.clip(result, -limit, limit).astype(kind)


def setup_inputs(seed: int = 0) -> dict:
    key_list = jax.random.split(jax.random.key(seed), 6)
    return {
        "embedding": draw_embedding(jax.random.fold_in(key_list[5], 71), 0),
        "subspace": bell_draw(key_list[1], (BLOCKS, R, K), 1.0, 6.0, ((0, 128),), jnp.float32),
        "degree": jnp.clip(jnp.exp(math.log(3000.0) - 2.3025851 * jax.random.uniform(key_list[2], (BLOCKS, R), jnp.float32) ** block_scale(key_list[2], (BLOCKS, R), ((0, 128),), -0.2, 0.2)), 300.0, 3000.0),
        "neighbours": draw_neighbours(jax.random.fold_in(key_list[5], 71), 0),
        "counts": draw_counts(jax.random.fold_in(key_list[5], 71), 0),
    }


def affinity(left, right, left_sq, right_sq):
    feature = left.shape[-1]
    cross = lax.dot_general(left.astype(jnp.float32), right.astype(jnp.float32), (((1,), (1,)), ((), ())), preferred_element_type=jnp.float32)
    distance = left_sq[:, None] + right_sq[None, :] - 2.0 * cross
    return jnp.exp((2.0 * feature - distance) / (4.0 * math.sqrt(feature))).astype(jnp.bfloat16)

def transposed(tile, values):
    return lax.dot_general(tile.astype(jnp.float32), values.astype(jnp.float32), (((0,), (0,)), ((), ())), preferred_element_type=jnp.float32)

def own_term(packed):
    block_x, block_sq, block_u = packed
    diagonal_mask = jnp.eye(block_x.shape[0], dtype=bool)
    tile = jnp.where(diagonal_mask, jnp.zeros((), jnp.bfloat16), affinity(block_x, block_x, block_sq, block_sq))
    return jnp.dot(tile.astype(jnp.float32), block_u.astype(jnp.float32), preferred_element_type=jnp.float32)

def reference(embedding, subspace, degree, neighbours, counts):
    total_blocks, block_rows, feature = embedding.shape
    group = BLK_DEV * N_BLK
    inv_root = 1.0 / jnp.sqrt(degree)
    scaled = (subspace * inv_root[..., None]).astype(jnp.bfloat16)
    squares = lax.optimization_barrier(jnp.sum(jnp.square(embedding.astype(jnp.float32)), axis=-1))
    product = lax.map(own_term, (embedding, squares, scaled))
    slot_total = neighbours.shape[1]

    def per_block(running, source):
        offset = source // group * group

        def per_slot(slot_id, running):
            target = offset + neighbours[source, slot_id]

            def compute(running):
                tile = affinity(embedding[source], embedding[target], squares[source], squares[target])
                running = running.at[source].add(jnp.dot(tile.astype(jnp.float32), scaled[target].astype(jnp.float32), preferred_element_type=jnp.float32))
                return running.at[target].add(transposed(tile, scaled[source]))
            return lax.cond(slot_id < counts[source], compute, lambda kept: kept, running)
        return (lax.fori_loop(0, slot_total, per_slot, running), None)
    product, _ = lax.scan(per_block, product, jnp.arange(total_blocks, dtype=jnp.int32))
    image = product * inv_root[..., None]
    flat = image.reshape(-1, image.shape[-1])
    gram = jnp.dot(flat.T, flat, precision=lax.Precision.HIGHEST) / (total_blocks * block_rows)
    lower = jnp.linalg.cholesky(gram)
    solved = jax.scipy.linalg.solve_triangular(lower, flat.T, lower=True)
    return solved.T.reshape(image.shape)
```

```python
import functools
import math

import jax
import jax.numpy as jnp
from jax import lax
from jax.experimental import pallas as pl
from jax.experimental.pallas import tpu as pltpu
from jax.sharding import PartitionSpec as P

ROWS = 256
FEAT = 1024
COLS = 64
OWN = 4
SIDE = 4
HALF = OWN // 2 * ROWS
DOCS = OWN * ROWS
META = 16
SCALED = 32
Z_ROWS = META + DOCS
Z_CUT = META + HALF
Y_X = SCALED + META
Y_ROWS = Y_X + DOCS + SCALED
Y_CUT = Y_X + HALF
LOG2E = 1.4426950408889634
GAIN = 2.0 * LOG2E / (4.0 * math.sqrt(FEAT))
BIAS = 2.0 * FEAT * LOG2E / (4.0 * math.sqrt(FEAT))
SQ_GAIN = -LOG2E / (4.0 * math.sqrt(FEAT))

NT = (((1,), (1,)), ((), ()))
NN = (((1,), (0,)), ((), ()))


def dot(a, b, dims):
    return lax.dot_general(a, b, dims, preferred_element_type=jnp.float32)


def prep_kernel(nbr_ref, cnt_ref, x_ref, sub_ref, deg_ref, py_ref, pz_ref, small, sems):
    copies = [
        pltpu.make_async_copy(x_ref, pz_ref.at[pl.ds(META, DOCS)], sems.at[0]),
        pltpu.make_async_copy(x_ref, py_ref.at[pl.ds(Y_X, DOCS)], sems.at[1]),
    ]
    for copy in copies:
        copy.start()
    lane = lax.broadcasted_iota(jnp.int32, (1, 128), 1)
    ones = jnp.ones((META, FEAT), jnp.bfloat16)
    squares = []
    adjacency = []
    for b in range(OWN):
        x = x_ref[b * ROWS:(b + 1) * ROWS, :].astype(jnp.float32)
        sq = x * x
        high = sq.astype(jnp.bfloat16)
        low = (sq - high.astype(jnp.float32)).astype(jnp.bfloat16)
        squares.append(dot(ones, high, NT) + dot(ones, low, NT))
        row = jnp.zeros((1, 128), jnp.float32)
        for k in range(nbr_ref.shape[1]):
            used = (k < cnt_ref[b]).astype(jnp.float32)
            row = row + jnp.where(lane == nbr_ref[b, k], used, 0.0)
        adjacency.append(row)
        inv = 1.0 / jnp.sqrt(deg_ref[b:b + 1, :])
        scaled = (sub_ref[b].T * inv).astype(jnp.bfloat16)
        packed = jnp.concatenate([scaled[16 * g:16 * (g + 1), :] for g in range(4)], axis=1)
        place = 16 * b if b < 2 else SCALED + META + 16 * (b - 2)
        small[place:place + 16, :] = packed
    total = jnp.concatenate(squares, axis=1)
    s_high = total.astype(jnp.bfloat16).astype(jnp.float32)
    rest = total - s_high
    s_mid = rest.astype(jnp.bfloat16).astype(jnp.float32)
    s_low = rest - s_mid
    which = lax.broadcasted_iota(jnp.int32, (META, FEAT), 0)
    meta = jnp.where(which == 0, s_high, jnp.where(which == 1, s_mid, jnp.where(which == 2, s_low, 0.0)))
    pad = jnp.zeros((1, FEAT - 128), jnp.float32)
    for b in range(OWN):
        wide = jnp.concatenate([adjacency[b], pad], axis=1)
        meta = jnp.where(which == 4 + b, wide, meta)
    small[SCALED:SCALED + META, :] = meta.astype(jnp.bfloat16)
    tail = [
        pltpu.make_async_copy(small.at[pl.ds(0, Y_X)], py_ref.at[pl.ds(0, Y_X)], sems.at[2]),
        pltpu.make_async_copy(small.at[pl.ds(Y_X, SCALED)], py_ref.at[pl.ds(Y_X + DOCS, SCALED)], sems.at[3]),
        pltpu.make_async_copy(small.at[pl.ds(SCALED, META)], pz_ref.at[pl.ds(0, META)], sems.at[4]),
    ]
    for copy in tail:
        copy.start()
    for copy in copies + tail:
        copy.wait()


def prepare(embedding, subspace, degree, neighbours, counts):
    smem = pl.BlockSpec(memory_space=pltpu.SMEM)
    vmem = pl.BlockSpec(memory_space=pltpu.VMEM)
    hbm = pl.BlockSpec(memory_space=pl.ANY)
    return pl.pallas_call(
        prep_kernel,
        out_shape=(
            jax.ShapeDtypeStruct((Y_ROWS, FEAT), jnp.bfloat16),
            jax.ShapeDtypeStruct((Z_ROWS, FEAT), jnp.bfloat16),
        ),
        in_specs=[smem, smem, vmem, vmem, vmem],
        out_specs=(hbm, hbm),
        scratch_shapes=[
            pltpu.VMEM((2 * SCALED + META, FEAT), jnp.bfloat16),
            pltpu.SemaphoreType.DMA((5,)),
        ],
        compiler_params=pltpu.CompilerParams(vmem_limit_bytes=24 * 2**20),
        name="prepare",
    )(neighbours, counts, embedding.reshape(DOCS, FEAT), subspace, degree)


def stage_kernel(second, *refs):
    slots = 16 if second else 12
    groups = slots // OWN
    n_side = 5 if second else 3
    idx_ref = refs[0]
    z_refs = refs[1:1 + n_side]
    y_refs = refs[1 + n_side:1 + 2 * n_side]
    rest = refs[1 + 2 * n_side:]
    if second:
        acc_in, rest = rest[0], rest[1:]
        outs, rest = rest[:4], rest[4:]
    else:
        acc_out, rest = rest[0], rest[1:]
    (r_x, c_x, c_s, c_pack, meta_r, meta_c, sq_r, sq_c, col, adj_vmem, adj_r, adj_c, acc,
     sem_r, sem_c, sem_s, sem_m, sem_a) = rest

    def source_z(group, half):
        if group < 3:
            return z_refs[group], META + half * HALF
        return (z_refs[3], META) if half == 0 else (z_refs[4], 0)

    def source_y(group, half):
        if group < 3:
            return y_refs[group], Y_X + half * HALF
        return (y_refs[3], Y_X) if half == 0 else (y_refs[4], 0)

    copies_m = []
    copies_s = []
    for g in range(groups):
        copies_m.append(pltpu.make_async_copy(z_refs[g].at[pl.ds(0, META)], meta_r.at[g], sem_m.at[g]))
        copies_m.append(pltpu.make_async_copy(y_refs[g].at[pl.ds(SCALED, META)], meta_c.at[g], sem_m.at[4 + g]))
        copies_s.append(pltpu.make_async_copy(y_refs[g].at[pl.ds(0, SCALED)], c_pack.at[g, pl.ds(0, SCALED)], sem_s.at[g]))
        far, start = (y_refs[g], Y_X + DOCS) if g < 3 else (y_refs[4], HALF)
        copies_s.append(pltpu.make_async_copy(far.at[pl.ds(start, SCALED)], c_pack.at[g, pl.ds(SCALED, SCALED)], sem_s.at[4 + g]))

    def copy_r(s):
        ref, start = source_z(s // OWN, s % OWN // 2)
        return pltpu.make_async_copy(ref.at[pl.ds(start + s % 2 * ROWS, ROWS)], r_x.at[s], sem_r.at[s])

    def copy_c(s):
        ref, start = source_y(s // OWN, s % OWN // 2)
        return pltpu.make_async_copy(ref.at[pl.ds(start + s % 2 * ROWS, ROWS)], c_x.at[s], sem_c.at[s])

    if second:
        pltpu.make_async_copy(acc_in, acc, sem_a.at[2]).start()
    for copy in copies_m:
        copy.start()
    first_r = range(12, 16) if second else range(12)
    for s in first_r:
        copy_r(s).start()
    copy_c(0).start()
    for copy in copies_s:
        copy.start()
    for s in range(1, slots):
        copy_c(s).start()
    if second:
        for s in range(12):
            copy_r(s).start()

    for copy in copies_m:
        copy.wait()
    for side, (meta, keep, adj) in enumerate(((meta_r, sq_r, adj_r), (meta_c, sq_c, adj_c))):
        for g in range(groups):
            m = meta[g].astype(jnp.float32)
            total = (m[0:1, :] + m[1:2, :] + m[2:3, :]) * SQ_GAIN
            if side == 0:
                total = total + BIAS
            for b in range(OWN):
                keep[g * OWN + b] = total[:, b * ROWS:(b + 1) * ROWS]
            adj_vmem[side, g * OWN:(g + 1) * OWN, :] = m[4:4 + OWN, 0:128].astype(jnp.int32)
        pltpu.make_async_copy(adj_vmem.at[side], adj, sem_a.at[side]).start()
    for copy in copies_s:
        copy.wait()
    for g in range(groups):
        for b in range(OWN):
            p = c_pack[g, 16 * b:16 * (b + 1), :]
            c_s[g * OWN + b] = jnp.concatenate([p[:, ROWS * k:ROWS * (k + 1)] for k in range(4)], axis=0)
    if second:
        pltpu.make_async_copy(acc_in, acc, sem_a.at[2]).wait()
    else:
        acc[...] = jnp.zeros_like(acc)
    for side, adj in enumerate((adj_r, adj_c)):
        pltpu.make_async_copy(adj_vmem.at[side], adj, sem_a.at[side]).wait()

    def body(c, r, weight, own):
        cross = dot(c_x[c], r_x[r], NT)
        tile = jnp.exp2(cross * GAIN + (jnp.concatenate([col[...], col[...]], axis=1) + sq_r[r])).astype(jnp.bfloat16)
        if own:
            row_id = lax.broadcasted_iota(jnp.int32, (ROWS, ROWS), 0)
            col_id = lax.broadcasted_iota(jnp.int32, (ROWS, ROWS), 1)
            tile = jnp.where(row_id == col_id, jnp.zeros_like(tile), tile)
        acc[r] = acc[r] + weight * dot(c_s[c], tile, NN)

    def sweep(c_lo, c_hi, r_lo, r_hi, wait_r):
        def per_c(c, carry):
            pltpu.make_async_copy(c_x.at[c], c_x.at[c], sem_c.at[c]).wait()
            col[...] = jnp.transpose(jnp.broadcast_to(sq_c[c], (128, ROWS)))
            block_c = idx_ref[1, c]

            def per_r(r, carry):
                @pl.when((c == c_lo) & (r >= wait_r[0]) & (r < wait_r[1]))
                def _():
                    pltpu.make_async_copy(r_x.at[r], r_x.at[r], sem_r.at[r]).wait()

                block_r = idx_ref[0, r]
                edges = adj_r[r, block_c] + adj_c[c, block_r]

                @pl.when(edges > 0)
                def _():
                    body(c, r, edges.astype(jnp.float32), False)

                if not second:
                    @pl.when(block_r == block_c)
                    def _():
                        body(c, r, 1.0, True)
                return carry

            return lax.fori_loop(r_lo, r_hi, per_r, carry)

        lax.fori_loop(c_lo, c_hi, per_c, 0)

    if second:
        sweep(0, 12, 12, 16, (12, 16))
        sweep(12, 16, 0, 16, (0, 12))
        for g in range(4):
            outs[g][...] = acc[g * OWN:(g + 1) * OWN]
    else:
        sweep(0, 12, 0, 12, (0, 12))
        acc_out[...] = acc[...]


def stage(second, index, z_parts, y_parts, acc=None):
    smem = pl.BlockSpec(memory_space=pltpu.SMEM)
    vmem = pl.BlockSpec(memory_space=pltpu.VMEM)
    hbm = pl.BlockSpec(memory_space=pl.ANY)
    slots = 16 if second else 12
    groups = slots // OWN
    operands = [index, *z_parts, *y_parts]
    in_specs = [smem] + [hbm] * (len(z_parts) + len(y_parts))
    if second:
        operands.append(acc)
        in_specs.append(hbm)
        out_shape = tuple(jax.ShapeDtypeStruct((OWN, COLS, ROWS), jnp.float32) for _ in range(4))
        out_specs = (vmem,) * 4
    else:
        out_shape = jax.ShapeDtypeStruct((16, COLS, ROWS), jnp.float32)
        out_specs = vmem
    return pl.pallas_call(
        functools.partial(stage_kernel, second),
        out_shape=out_shape,
        in_specs=in_specs,
        out_specs=out_specs,
        scratch_shapes=[
            pltpu.VMEM((slots, ROWS, FEAT), jnp.bfloat16),
            pltpu.VMEM((slots, ROWS, FEAT), jnp.bfloat16),
            pltpu.VMEM((slots, COLS, ROWS), jnp.bfloat16),
            pltpu.VMEM((groups, 2 * SCALED, FEAT), jnp.bfloat16),
            pltpu.VMEM((groups, META, FEAT), jnp.bfloat16),
            pltpu.VMEM((groups, META, FEAT), jnp.bfloat16),
            pltpu.VMEM((slots, 1, ROWS), jnp.float32),
            pltpu.VMEM((slots, 1, ROWS), jnp.float32),
            pltpu.VMEM((ROWS, 128), jnp.float32),
            pltpu.VMEM((2, 16, 128), jnp.int32),
            pltpu.SMEM((16, 128), jnp.int32),
            pltpu.SMEM((16, 128), jnp.int32),
            pltpu.VMEM((16, COLS, ROWS), jnp.float32),
            pltpu.SemaphoreType.DMA((16,)),
            pltpu.SemaphoreType.DMA((16,)),
            pltpu.SemaphoreType.DMA((8,)),
            pltpu.SemaphoreType.DMA((8,)),
            pltpu.SemaphoreType.DMA((3,)),
        ],
        compiler_params=pltpu.CompilerParams(vmem_limit_bytes=32 * 2**20),
        cost_estimate=pl.CostEstimate(flops=6 * 10**9, bytes_accessed=16 * 2**20, transcendentals=10**6),
        name="stage_two" if second else "stage_one",
    )(*operands)


def finish_kernel(deg_ref, own_ref, a_ref, b_ref, c_ref, image_ref, gram_ref):
    parts = []
    for b in range(OWN):
        inv = 1.0 / jnp.sqrt(deg_ref[b:b + 1, :])
        parts.append((own_ref[b] + a_ref[b] + (b_ref[b] + c_ref[b])) * inv)
    image = jnp.concatenate(parts, axis=1)
    image_ref[...] = image
    gram_ref[...] = lax.dot_general(
        image, image, NT, precision=lax.Precision.HIGHEST, preferred_element_type=jnp.float32
    )


def finish(degree, own, a, b, c):
    return pl.pallas_call(
        finish_kernel,
        out_shape=(
            jax.ShapeDtypeStruct((COLS, DOCS), jnp.float32),
            jax.ShapeDtypeStruct((COLS, COLS), jnp.float32),
        ),
        name="finish",
    )(degree, own, a, b, c)


def shift_z(k):
    return [(y * SIDE + z, y * SIDE + (z + k) % SIDE) for y in range(SIDE) for z in range(SIDE)]


def shift_y(k):
    return [(y * SIDE + z, (y + k) % SIDE * SIDE + z) for y in range(SIDE) for z in range(SIDE)]


def per_device(embedding, subspace, degree, neighbours, counts):
    position = lax.axis_index("blk")
    y, z = position // SIDE, position % SIDE
    order = (0, SIDE - 1, 1, 2)
    row_ids = jnp.stack([(y * SIDE + (z + k) % SIDE) * OWN + b for k in order for b in range(OWN)])
    col_ids = jnp.stack([((y + k) % SIDE * SIDE + z) * OWN + b for k in order for b in range(OWN)])
    index = jnp.stack([row_ids, col_ids]).astype(jnp.int32)

    pack_y, pack_z = prepare(embedding, subspace, degree, neighbours, counts)
    z_minus = lax.ppermute(pack_z, "blk", shift_z(1))
    z_plus = lax.ppermute(pack_z, "blk", shift_z(-1))
    y_minus = lax.ppermute(pack_y, "blk", shift_y(1))
    y_plus = lax.ppermute(pack_y, "blk", shift_y(-1))
    z_far_a = lax.ppermute(z_minus[:Z_CUT], "blk", shift_z(1))
    z_far_b = lax.ppermute(z_plus[Z_CUT:], "blk", shift_z(-1))
    y_far_a = lax.ppermute(y_minus[:Y_CUT], "blk", shift_y(1))
    y_far_b = lax.ppermute(y_plus[Y_CUT:], "blk", shift_y(-1))

    near_z = (pack_z, z_minus, z_plus)
    near_y = (pack_y, y_minus, y_plus)
    acc = stage(False, index, near_z, near_y)
    own, to_minus, to_plus, to_far = stage(
        True, index, near_z + (z_far_a, z_far_b), near_y + (y_far_a, y_far_b), acc
    )
    back_a = lax.ppermute(to_minus, "blk", shift_z(-1))
    back_b = lax.ppermute(to_plus, "blk", shift_z(1))
    back_c = lax.ppermute(to_far, "blk", shift_z(2))
    image, gram = finish(degree, own, back_a, back_b, back_c)

    devices_blk = lax.axis_size("blk")
    devices_dp = lax.axis_size("dp")
    step = 1
    while step < devices_blk:
        gram = gram + lax.ppermute(gram, "blk", [(i, i ^ step) for i in range(devices_blk)])
        step *= 2
    step = 1
    while step < devices_dp:
        gram = gram + lax.ppermute(gram, "dp", [(i, i ^ step) for i in range(devices_dp)])
        step *= 2
    gram = gram / (DOCS * devices_blk * devices_dp)
    lower = jnp.linalg.cholesky(gram)
    solved = jax.scipy.linalg.solve_triangular(lower, image, lower=True)
    return solved.T.reshape(OWN, ROWS, COLS)


def solution(mesh):
    placed = (
        P(("dp", "blk"), None, None),
        P(("dp", "blk"), None, None),
        P(("dp", "blk"), None),
        P(("dp", "blk"), None),
        P(("dp", "blk")),
    )
    return jax.shard_map(
        per_device,
        mesh=mesh,
        in_specs=placed,
        out_specs=P(("dp", "blk"), None, None),
        check_vma=False,
    )
```

```python
import functools
import math

import jax
import jax.numpy as jnp
from jax import lax
from jax.experimental import pallas as pl
from jax.experimental.pallas import tpu as pltpu
from jax.sharding import PartitionSpec as P

ROWS = 256
FEAT = 1024
COLS = 64
OWN = 4
SIDE = 4
HALF = OWN // 2 * ROWS
DOCS = OWN * ROWS
META = 16
SCALED = 32
UNIT = 2
UNITS = 2 * SIDE
Z_ROWS = META + HALF
Y_X = SCALED + META
Y_ROWS = Y_X + HALF
GROUPED = 4
VMEM_LIMIT = 62 * 2**20
ARRIVAL = ((0, 0), (0, 1), (-1, 0), (1, 1), (-1, 1), (1, 0), (2, 0), (2, 1))
LOG2E = 1.4426950408889634
GAIN = 2.0 * LOG2E / (4.0 * math.sqrt(FEAT))
BIAS = 2.0 * FEAT * LOG2E / (4.0 * math.sqrt(FEAT))
SQ_GAIN = -LOG2E / (4.0 * math.sqrt(FEAT))

NT = (((1,), (1,)), ((), ()))
NN = (((1,), (0,)), ((), ()))


def dot(a, b, dims):
    return lax.dot_general(a, b, dims, preferred_element_type=jnp.float32)


def prep_kernel(nbr_hbm, cnt_hbm, x_hbm, sub_hbm, deg_hbm, za_ref, zb_ref, ya_ref, yb_ref,
                nbr_ref, cnt_ref, x_ref, sub_ref, deg_ref, small, sems):
    loads = [
        pltpu.make_async_copy(x_hbm.at[pl.ds(b * ROWS, ROWS)], x_ref.at[pl.ds(b * ROWS, ROWS)], sems.at[b])
        for b in range(OWN)
    ]
    extra = [
        pltpu.make_async_copy(nbr_hbm, nbr_ref, sems.at[4]),
        pltpu.make_async_copy(cnt_hbm, cnt_ref, sems.at[5]),
        pltpu.make_async_copy(deg_hbm, deg_ref, sems.at[6]),
        pltpu.make_async_copy(sub_hbm, sub_ref, sems.at[7]),
    ]
    for copy in loads + extra:
        copy.start()
    stores = []

    def store(source, target, which):
        copy = pltpu.make_async_copy(source, target, sems.at[which])
        copy.start()
        stores.append(copy)

    ones = jnp.ones((META, FEAT), jnp.bfloat16)
    squares = []
    for b in range(OWN):
        half, place = b // UNIT, b % UNIT * ROWS
        loads[b].wait()
        source = x_ref.at[pl.ds(b * ROWS, ROWS)]
        store(source, (za_ref, zb_ref)[half].at[pl.ds(META + place, ROWS)], 8 + b)
        store(source, (ya_ref, yb_ref)[half].at[pl.ds(Y_X + place, ROWS)], 12 + b)
        x = x_ref[b * ROWS:(b + 1) * ROWS, :].astype(jnp.float32)
        sq = x * x
        high = sq.astype(jnp.bfloat16)
        low = (sq - high.astype(jnp.float32)).astype(jnp.bfloat16)
        squares.append(dot(ones, high, NT) + dot(ones, low, NT))
    for copy in extra:
        copy.wait()
    lane = lax.broadcasted_iota(jnp.int32, (1, 128), 1)
    which = lax.broadcasted_iota(jnp.int32, (META, FEAT), 0)
    pad = jnp.zeros((1, FEAT - 128), jnp.float32)
    for half in range(2):
        total = jnp.concatenate(squares[half * UNIT:(half + 1) * UNIT] + [jnp.zeros((META, FEAT - HALF), jnp.float32)], axis=1)
        s_high = total.astype(jnp.bfloat16).astype(jnp.float32)
        rest = total - s_high
        s_mid = rest.astype(jnp.bfloat16).astype(jnp.float32)
        s_low = rest - s_mid
        meta = jnp.where(which == 0, s_high, jnp.where(which == 1, s_mid, jnp.where(which == 2, s_low, 0.0)))
        for i in range(UNIT):
            b = half * UNIT + i
            row = jnp.zeros((1, 128), jnp.float32)
            for k in range(nbr_ref.shape[1]):
                used = (k < cnt_ref[b]).astype(jnp.float32)
                row = row + jnp.where(lane == nbr_ref[b, k], used, 0.0)
            meta = jnp.where(which == 4 + i, jnp.concatenate([row, pad], axis=1), meta)
            inv = 1.0 / jnp.sqrt(deg_ref[b:b + 1, :])
            scaled = (sub_ref[b] * inv).astype(jnp.bfloat16)
            small[half, 16 * i:16 * (i + 1), :] = jnp.concatenate(
                [scaled[16 * g:16 * (g + 1), :] for g in range(4)], axis=1
            )
        small[half, SCALED:Y_X, :] = meta.astype(jnp.bfloat16)
        store(small.at[half], (ya_ref, yb_ref)[half].at[pl.ds(0, Y_X)], 16 + half)
        store(small.at[half, pl.ds(SCALED, META)], (za_ref, zb_ref)[half].at[pl.ds(0, META)], 18 + half)
    for copy in stores:
        copy.wait()


def prepare(embedding, subspace, degree, neighbours, counts):
    hbm = pl.BlockSpec(memory_space=pltpu.HBM)
    return pl.pallas_call(
        prep_kernel,
        out_shape=(jax.ShapeDtypeStruct((Z_ROWS, FEAT), jnp.bfloat16),) * 2
        + (jax.ShapeDtypeStruct((Y_ROWS, FEAT), jnp.bfloat16),) * 2,
        in_specs=[hbm] * 5,
        out_specs=(hbm,) * 4,
        scratch_shapes=[
            pltpu.SMEM(neighbours.shape, jnp.int32),
            pltpu.SMEM(counts.shape, jnp.int32),
            pltpu.VMEM((DOCS, FEAT), jnp.bfloat16),
            pltpu.VMEM((OWN, COLS, ROWS), jnp.float32),
            pltpu.VMEM((OWN, ROWS), jnp.float32),
            pltpu.VMEM((2, Y_X, FEAT), jnp.bfloat16),
            pltpu.SemaphoreType.DMA((20,)),
        ],
        compiler_params=pltpu.CompilerParams(vmem_limit_bytes=VMEM_LIMIT),
        name="prepare",
    )(neighbours, counts, embedding.reshape(DOCS, FEAT), jnp.swapaxes(subspace, 1, 2), degree)


def stage_kernel(old, new, last, *refs):
    idx_ref = refs[0]
    z_refs = refs[1:1 + new]
    y_refs = refs[1 + new:1 + 2 * new]
    rest = refs[1 + 2 * new:]
    if old:
        acc_in, rest = rest[0], rest[1:]
    if last:
        outs, rest = rest[:4], rest[4:]
    else:
        acc_out, rest = rest[0], rest[1:]
    (r_x, c_x, c_s, c_pack, meta_r, meta_c, sq_r, sq_c, col, adj_vmem, adj_r, adj_c, codes, edge_list, acc,
     sem_r, sem_c, sem_s, sem_m, sem_n, sem_a) = rest
    old_slots, slots = UNIT * old, UNIT * new

    meta_copies = []
    pack_copies = []
    r_copies = []
    c_copies = []
    for u in range(new):
        meta_copies.append(pltpu.make_async_copy(z_refs[u].at[pl.ds(0, META)], meta_r.at[u], sem_m.at[u]))
        meta_copies.append(pltpu.make_async_copy(y_refs[u].at[pl.ds(SCALED, META)], meta_c.at[u], sem_n.at[u]))
        pack_copies.append(pltpu.make_async_copy(y_refs[u].at[pl.ds(0, SCALED)], c_pack.at[u], sem_s.at[u]))
        r_copies.append(pltpu.make_async_copy(z_refs[u].at[pl.ds(META, HALF)], r_x.at[u], sem_r.at[u]))
        c_copies.append(pltpu.make_async_copy(y_refs[u].at[pl.ds(Y_X, HALF)], c_x.at[u], sem_c.at[u]))
    if old:
        acc_copy = pltpu.make_async_copy(acc_in, acc, sem_a.at[2])
    for copy in meta_copies:
        copy.start()
    for copy in r_copies[old:] + c_copies[:old] + pack_copies:
        copy.start()
    if old:
        acc_copy.start()
    for copy in c_copies[old:] + r_copies[:old]:
        copy.start()

    for copy in meta_copies:
        copy.wait()
    for side, (meta, keep, adj) in enumerate(((meta_r, sq_r, adj_r), (meta_c, sq_c, adj_c))):
        for u in range(new):
            m = meta[u].astype(jnp.float32)
            total = (m[0:1, 0:HALF] + m[1:2, 0:HALF] + m[2:3, 0:HALF]) * SQ_GAIN
            for i in range(UNIT):
                piece = total[:, i * ROWS:(i + 1) * ROWS]
                if side == 0:
                    keep[u * UNIT + i] = piece + BIAS
                else:
                    keep[u * UNIT + i:u * UNIT + i + 1, :] = piece
            adj_vmem[side, u * UNIT:(u + 1) * UNIT, :] = m[4:4 + UNIT, 0:128].astype(jnp.int32)
        pltpu.make_async_copy(adj_vmem.at[side], adj, sem_a.at[side]).start()
    columns = jnp.transpose(sq_c[...])
    for s in range(slots):
        col[s] = jnp.broadcast_to(columns[:, s:s + 1], (ROWS, 128))
    for copy in pack_copies:
        copy.wait()
    for s in range(slots):
        p = c_pack[s // UNIT, 16 * (s % UNIT):16 * (s % UNIT + 1), :]
        c_s[s] = jnp.concatenate([p[:, ROWS * k:ROWS * (k + 1)] for k in range(4)], axis=0)
    for side, adj in enumerate((adj_r, adj_c)):
        pltpu.make_async_copy(adj_vmem.at[side], adj, sem_a.at[side]).wait()

    def form(pairs, diagonal):
        cross = [
            dot(c_x[c // UNIT, pl.ds(c % UNIT * ROWS, ROWS), :], r_x[r // UNIT, pl.ds(r % UNIT * ROWS, ROWS), :], NT)
            for c, r, _ in pairs
        ]
        terms = []
        for (c, r, weight), value in zip(pairs, cross):
            bias = jnp.concatenate([col[c], col[c]], axis=1) + sq_r[r]
            tile = jnp.exp2(value * GAIN + bias)
            if diagonal:
                row_id = lax.broadcasted_iota(jnp.int32, (ROWS, ROWS), 0)
                col_id = lax.broadcasted_iota(jnp.int32, (ROWS, ROWS), 1)
                tile = jnp.where(row_id == col_id, 0.0, tile)
            term = dot(c_s[c], tile.astype(jnp.bfloat16), NN)
            terms.append(term if diagonal else term * weight)
        for (c, r, _), term in zip(pairs, terms):
            acc[r] = acc[r] + term

    def list_tiles(c_lo, c_hi, r_lo, r_hi):
        def per_c(c, count):
            block_c = idx_ref[1, c]
            for r in range(r_lo, r_hi):
                edges = adj_r[r, block_c] + adj_c[c, idx_ref[0, r]]
                codes[count] = c * 16 + r
                edge_list[count] = edges
                count = count + (edges > 0).astype(jnp.int32)
            return count

        count = lax.fori_loop(c_lo, c_hi, per_c, 0)
        for i in range(GROUPED - 1):
            codes[count + i] = codes[0]
            edge_list[count + i] = 0
        return count

    def run_tiles(count):
        def step(t, carry):
            pairs = []
            for i in range(GROUPED):
                code = codes[t * GROUPED + i]
                pairs.append((code // 16, code % 16, edge_list[t * GROUPED + i].astype(jnp.float32)))
            form(pairs, False)
            return carry

        lax.fori_loop(0, (count + GROUPED - 1) // GROUPED, step, 0)

    if old:
        count = list_tiles(0, old_slots, old_slots, slots)
        for copy in [acc_copy] + r_copies[old:] + c_copies[:old]:
            copy.wait()
        run_tiles(count)
        count = list_tiles(old_slots, slots, 0, slots)
        for copy in c_copies[old:] + r_copies[:old]:
            copy.wait()
        run_tiles(count)
    else:
        acc[...] = jnp.zeros_like(acc)
        count = list_tiles(0, slots, 0, slots)
        for copy in c_copies + r_copies:
            copy.wait()
        form([(s, s, None) for s in range(OWN)], True)
        run_tiles(count)
    if last:
        for out, order in zip(outs, ((0, 1, 2, 3), (4, 5, 8, 9), (10, 11, 6, 7), (12, 13, 14, 15))):
            for k, s in enumerate(order):
                out[k] = acc[s]
    else:
        acc_out[...] = acc[...]


def stage(old, new, index, z_parts, y_parts, acc=None):
    smem = pl.BlockSpec(memory_space=pltpu.SMEM)
    vmem = pl.BlockSpec(memory_space=pltpu.VMEM)
    hbm = pl.BlockSpec(memory_space=pltpu.HBM)
    last = new == UNITS
    operands = [index, *z_parts[:new], *y_parts[:new]]
    in_specs = [smem] + [hbm] * (2 * new)
    if old:
        operands.append(acc)
        in_specs.append(hbm)
    if last:
        out_shape = tuple(jax.ShapeDtypeStruct((OWN, COLS, ROWS), jnp.float32) for _ in range(4))
        out_specs = (vmem,) * 4
    else:
        out_shape = jax.ShapeDtypeStruct((16, COLS, ROWS), jnp.float32)
        out_specs = vmem
    slots = UNIT * new
    return pl.pallas_call(
        functools.partial(stage_kernel, old, new, last),
        out_shape=out_shape,
        in_specs=in_specs,
        out_specs=out_specs,
        scratch_shapes=[
            pltpu.VMEM((new, HALF, FEAT), jnp.bfloat16),
            pltpu.VMEM((new, HALF, FEAT), jnp.bfloat16),
            pltpu.VMEM((slots, COLS, ROWS), jnp.bfloat16),
            pltpu.VMEM((new, SCALED, FEAT), jnp.bfloat16),
            pltpu.VMEM((new, META, FEAT), jnp.bfloat16),
            pltpu.VMEM((new, META, FEAT), jnp.bfloat16),
            pltpu.VMEM((slots, 1, ROWS), jnp.float32),
            pltpu.VMEM((128, ROWS), jnp.float32),
            pltpu.VMEM((slots, ROWS, 128), jnp.float32),
            pltpu.VMEM((2, 16, 128), jnp.int32),
            pltpu.SMEM((16, 128), jnp.int32),
            pltpu.SMEM((16, 128), jnp.int32),
            pltpu.SMEM((264,), jnp.int32),
            pltpu.SMEM((264,), jnp.int32),
            pltpu.VMEM((16, COLS, ROWS), jnp.float32),
            pltpu.SemaphoreType.DMA((new,)),
            pltpu.SemaphoreType.DMA((new,)),
            pltpu.SemaphoreType.DMA((new,)),
            pltpu.SemaphoreType.DMA((new,)),
            pltpu.SemaphoreType.DMA((new,)),
            pltpu.SemaphoreType.DMA((3,)),
        ],
        compiler_params=pltpu.CompilerParams(vmem_limit_bytes=VMEM_LIMIT),
        cost_estimate=pl.CostEstimate(flops=6 * 10**9, bytes_accessed=16 * 2**20, transcendentals=10**6),
        name="stage_%d" % new,
    )(*operands)


def finish_kernel(deg_ref, own_ref, a_ref, b_ref, c_ref, image_ref, gram_ref):
    parts = []
    for b in range(OWN):
        inv = 1.0 / jnp.sqrt(deg_ref[b:b + 1, :])
        parts.append((own_ref[b] + a_ref[b] + (b_ref[b] + c_ref[b])) * inv)
    image = jnp.concatenate(parts, axis=1)
    image_ref[...] = image
    gram_ref[...] = lax.dot_general(
        image, image, NT, precision=lax.Precision.HIGHEST, preferred_element_type=jnp.float32
    )


def finish(degree, own, a, b, c):
    return pl.pallas_call(
        finish_kernel,
        out_shape=(
            jax.ShapeDtypeStruct((COLS, DOCS), jnp.float32),
            jax.ShapeDtypeStruct((COLS, COLS), jnp.float32),
        ),
        compiler_params=pltpu.CompilerParams(vmem_limit_bytes=VMEM_LIMIT),
        name="finish",
    )(degree, own, a, b, c)


def shift_z(k):
    return [(y * SIDE + z, y * SIDE + (z + k) % SIDE) for y in range(SIDE) for z in range(SIDE)]


def shift_y(k):
    return [(y * SIDE + z, (y + k) % SIDE * SIDE + z) for y in range(SIDE) for z in range(SIDE)]


def per_device(embedding, subspace, degree, neighbours, counts):
    position = lax.axis_index("blk")
    y, z = position // SIDE, position % SIDE
    row_ids = jnp.stack([(y * SIDE + (z + k) % SIDE) * OWN + UNIT * h + i for k, h in ARRIVAL for i in range(UNIT)])
    col_ids = jnp.stack([((y + k) % SIDE * SIDE + z) * OWN + UNIT * h + i for k, h in ARRIVAL for i in range(UNIT)])
    index = jnp.stack([row_ids, col_ids]).astype(jnp.int32)

    z_a, z_b, y_a, y_b = prepare(embedding, subspace, degree, neighbours, counts)

    def gather(a, b, shift):
        minus_a = lax.ppermute(a, "blk", shift(1))
        plus_b = lax.ppermute(b, "blk", shift(-1))
        b_next, minus_a = lax.optimization_barrier((b, minus_a))
        a_next, plus_b = lax.optimization_barrier((a, plus_b))
        minus_b = lax.ppermute(b_next, "blk", shift(1))
        plus_a = lax.ppermute(a_next, "blk", shift(-1))
        minus_next, minus_b = lax.optimization_barrier((minus_a, minus_b))
        plus_next, plus_a = lax.optimization_barrier((plus_b, plus_a))
        far_a = lax.ppermute(minus_next, "blk", shift(1))
        far_b = lax.ppermute(plus_next, "blk", shift(-1))
        return a, b, minus_a, plus_b, minus_b, plus_a, far_a, far_b

    z_parts = gather(z_a, z_b, shift_z)
    y_parts = gather(y_a, y_b, shift_y)
    acc = stage(0, 4, index, z_parts, y_parts)
    acc = stage(4, 6, index, z_parts, y_parts, acc)
    own, to_minus, to_plus, to_far = stage(6, 8, index, z_parts, y_parts, acc)
    back_a = lax.ppermute(to_minus, "blk", shift_z(-1))
    back_b = lax.ppermute(to_plus, "blk", shift_z(1))
    back_c = lax.ppermute(to_far, "blk", shift_z(2))
    image, gram = finish(degree, own, back_a, back_b, back_c)

    devices_blk = lax.axis_size("blk")
    devices_dp = lax.axis_size("dp")
    step = 1
    while step < devices_blk:
        gram = gram + lax.ppermute(gram, "blk", [(i, i ^ step) for i in range(devices_blk)])
        step *= 2
    step = 1
    while step < devices_dp:
        gram = gram + lax.ppermute(gram, "dp", [(i, i ^ step) for i in range(devices_dp)])
        step *= 2
    gram = gram / (DOCS * devices_blk * devices_dp)
    lower = jnp.linalg.cholesky(gram)
    solved = jax.scipy.linalg.solve_triangular(lower, image, lower=True)
    return solved.T.reshape(OWN, ROWS, COLS)


def solution(mesh):
    placed = (
        P(("dp", "blk"), None, None),
        P(("dp", "blk"), None, None),
        P(("dp", "blk"), None),
        P(("dp", "blk"), None),
        P(("dp", "blk")),
    )
    return jax.shard_map(
        per_device,
        mesh=mesh,
        in_specs=placed,
        out_specs=P(("dp", "blk"), None, None),
        check_vma=False,
    )
```

```python
import functools
import math

import jax
import jax.numpy as jnp
from jax import lax
from jax.experimental import pallas as pl
from jax.experimental.pallas import tpu as pltpu
from jax.sharding import PartitionSpec as P

ROWS = 256
FEAT = 1024
COLS = 64
OWN = 4
SIDE = 4
HALF = OWN // 2 * ROWS
DOCS = OWN * ROWS
META = 16
SCALED = 32
UNIT = 2
UNITS = 2 * SIDE
Z_ROWS = META + HALF
Y_X = SCALED + META
Y_ROWS = Y_X + HALF
GROUPED = 4
VMEM_LIMIT = 62 * 2**20
SMALL_LIMIT = 16 * 2**20
PANEL = 8
ARRIVAL = ((0, 0), (0, 1), (-1, 0), (1, 1), (-1, 1), (1, 0), (2, 0), (2, 1))
LOG2E = 1.4426950408889634
GAIN = 2.0 * LOG2E / (4.0 * math.sqrt(FEAT))
BIAS = 2.0 * FEAT * LOG2E / (4.0 * math.sqrt(FEAT))
SQ_GAIN = -LOG2E / (4.0 * math.sqrt(FEAT))

NT = (((1,), (1,)), ((), ()))
NN = (((1,), (0,)), ((), ()))


def dot(a, b, dims):
    return lax.dot_general(a, b, dims, preferred_element_type=jnp.float32)


def prep_kernel(nbr_hbm, cnt_hbm, x_hbm, sub_hbm, deg_hbm, za_ref, zb_ref, ya_ref, yb_ref,
                nbr_ref, cnt_ref, x_ref, sub_ref, deg_ref, small, sems):
    loads = [
        pltpu.make_async_copy(x_hbm.at[pl.ds(b * ROWS, ROWS)], x_ref.at[pl.ds(b * ROWS, ROWS)], sems.at[b])
        for b in range(OWN)
    ]
    extra = [
        pltpu.make_async_copy(nbr_hbm, nbr_ref, sems.at[4]),
        pltpu.make_async_copy(cnt_hbm, cnt_ref, sems.at[5]),
        pltpu.make_async_copy(deg_hbm, deg_ref, sems.at[6]),
        pltpu.make_async_copy(sub_hbm, sub_ref, sems.at[7]),
    ]
    for copy in loads + extra:
        copy.start()
    stores = []

    def store(source, target, which):
        copy = pltpu.make_async_copy(source, target, sems.at[which])
        copy.start()
        stores.append(copy)

    ones = jnp.ones((META, FEAT), jnp.bfloat16)
    squares = []
    for b in range(OWN):
        half, place = b // UNIT, b % UNIT * ROWS
        loads[b].wait()
        source = x_ref.at[pl.ds(b * ROWS, ROWS)]
        store(source, (za_ref, zb_ref)[half].at[pl.ds(META + place, ROWS)], 8 + b)
        store(source, (ya_ref, yb_ref)[half].at[pl.ds(Y_X + place, ROWS)], 12 + b)
        x = x_ref[b * ROWS:(b + 1) * ROWS, :].astype(jnp.float32)
        sq = x * x
        high = sq.astype(jnp.bfloat16)
        low = (sq - high.astype(jnp.float32)).astype(jnp.bfloat16)
        squares.append(dot(ones, high, NT) + dot(ones, low, NT))
    for copy in extra:
        copy.wait()
    lane = lax.broadcasted_iota(jnp.int32, (1, 128), 1)
    which = lax.broadcasted_iota(jnp.int32, (META, FEAT), 0)
    pad = jnp.zeros((1, FEAT - 128), jnp.float32)
    for half in range(2):
        total = jnp.concatenate(squares[half * UNIT:(half + 1) * UNIT] + [jnp.zeros((META, FEAT - HALF), jnp.float32)], axis=1)
        s_high = total.astype(jnp.bfloat16).astype(jnp.float32)
        rest = total - s_high
        s_mid = rest.astype(jnp.bfloat16).astype(jnp.float32)
        s_low = rest - s_mid
        meta = jnp.where(which == 0, s_high, jnp.where(which == 1, s_mid, jnp.where(which == 2, s_low, 0.0)))
        for i in range(UNIT):
            b = half * UNIT + i
            row = jnp.zeros((1, 128), jnp.float32)
            for k in range(nbr_ref.shape[1]):
                used = (k < cnt_ref[b]).astype(jnp.float32)
                row = row + jnp.where(lane == nbr_ref[b, k], used, 0.0)
            meta = jnp.where(which == 4 + i, jnp.concatenate([row, pad], axis=1), meta)
            inv = 1.0 / jnp.sqrt(deg_ref[b:b + 1, :])
            scaled = (sub_ref[b] * inv).astype(jnp.bfloat16)
            small[half, 16 * i:16 * (i + 1), :] = jnp.concatenate(
                [scaled[16 * g:16 * (g + 1), :] for g in range(4)], axis=1
            )
        small[half, SCALED:Y_X, :] = meta.astype(jnp.bfloat16)
        store(small.at[half], (ya_ref, yb_ref)[half].at[pl.ds(0, Y_X)], 16 + half)
        store(small.at[half, pl.ds(SCALED, META)], (za_ref, zb_ref)[half].at[pl.ds(0, META)], 18 + half)
    for copy in stores:
        copy.wait()


def prepare(embedding, subspace, degree, neighbours, counts):
    hbm = pl.BlockSpec(memory_space=pltpu.HBM)
    return pl.pallas_call(
        prep_kernel,
        out_shape=(jax.ShapeDtypeStruct((Z_ROWS, FEAT), jnp.bfloat16),) * 2
        + (jax.ShapeDtypeStruct((Y_ROWS, FEAT), jnp.bfloat16),) * 2,
        in_specs=[hbm] * 5,
        out_specs=(hbm,) * 4,
        scratch_shapes=[
            pltpu.SMEM(neighbours.shape, jnp.int32),
            pltpu.SMEM(counts.shape, jnp.int32),
            pltpu.VMEM((DOCS, FEAT), jnp.bfloat16),
            pltpu.VMEM((OWN, COLS, ROWS), jnp.float32),
            pltpu.VMEM((OWN, ROWS), jnp.float32),
            pltpu.VMEM((2, Y_X, FEAT), jnp.bfloat16),
            pltpu.SemaphoreType.DMA((20,)),
        ],
        compiler_params=pltpu.CompilerParams(vmem_limit_bytes=VMEM_LIMIT),
        name="prepare",
    )(neighbours, counts, embedding.reshape(DOCS, FEAT), jnp.swapaxes(subspace, 1, 2), degree)


def stage_kernel(old, new, last, *refs):
    idx_ref = refs[0]
    z_refs = refs[1:1 + new]
    y_refs = refs[1 + new:1 + 2 * new]
    rest = refs[1 + 2 * new:]
    if old:
        acc_in, rest = rest[0], rest[1:]
    if last:
        outs, rest = rest[:4], rest[4:]
    else:
        acc_out, rest = rest[0], rest[1:]
    (r_x, c_x, c_s, c_pack, meta_r, meta_c, sq_r, sq_c, col, adj_vmem, adj_r, adj_c, codes, edge_list, acc,
     sem_r, sem_c, sem_s, sem_m, sem_n, sem_a) = rest
    old_slots, slots = UNIT * old, UNIT * new

    meta_copies = []
    pack_copies = []
    r_copies = []
    c_copies = []
    for u in range(new):
        meta_copies.append(pltpu.make_async_copy(z_refs[u].at[pl.ds(0, META)], meta_r.at[u], sem_m.at[u]))
        meta_copies.append(pltpu.make_async_copy(y_refs[u].at[pl.ds(SCALED, META)], meta_c.at[u], sem_n.at[u]))
        pack_copies.append(pltpu.make_async_copy(y_refs[u].at[pl.ds(0, SCALED)], c_pack.at[u], sem_s.at[u]))
        r_copies.append(pltpu.make_async_copy(z_refs[u].at[pl.ds(META, HALF)], r_x.at[u], sem_r.at[u]))
        c_copies.append(pltpu.make_async_copy(y_refs[u].at[pl.ds(Y_X, HALF)], c_x.at[u], sem_c.at[u]))
    if old:
        acc_copy = pltpu.make_async_copy(acc_in, acc, sem_a.at[2])
    for copy in meta_copies:
        copy.start()
    for copy in r_copies[old:] + c_copies[:old] + pack_copies:
        copy.start()
    if old:
        acc_copy.start()
    for copy in c_copies[old:] + r_copies[:old]:
        copy.start()

    for copy in meta_copies:
        copy.wait()
    for side, (meta, keep, adj) in enumerate(((meta_r, sq_r, adj_r), (meta_c, sq_c, adj_c))):
        for u in range(new):
            m = meta[u].astype(jnp.float32)
            total = (m[0:1, 0:HALF] + m[1:2, 0:HALF] + m[2:3, 0:HALF]) * SQ_GAIN
            for i in range(UNIT):
                piece = total[:, i * ROWS:(i + 1) * ROWS]
                if side == 0:
                    keep[u * UNIT + i] = piece + BIAS
                else:
                    keep[u * UNIT + i:u * UNIT + i + 1, :] = piece
            adj_vmem[side, u * UNIT:(u + 1) * UNIT, :] = m[4:4 + UNIT, 0:128].astype(jnp.int32)
        pltpu.make_async_copy(adj_vmem.at[side], adj, sem_a.at[side]).start()
    columns = jnp.transpose(sq_c[...])
    for s in range(slots):
        col[s] = jnp.broadcast_to(columns[:, s:s + 1], (ROWS, 128))
    for copy in pack_copies:
        copy.wait()
    for s in range(slots):
        p = c_pack[s // UNIT, 16 * (s % UNIT):16 * (s % UNIT + 1), :]
        c_s[s] = jnp.concatenate([p[:, ROWS * k:ROWS * (k + 1)] for k in range(4)], axis=0)
    for side, adj in enumerate((adj_r, adj_c)):
        pltpu.make_async_copy(adj_vmem.at[side], adj, sem_a.at[side]).wait()

    def form(pairs, diagonal):
        cross = [
            dot(c_x[c // UNIT, pl.ds(c % UNIT * ROWS, ROWS), :], r_x[r // UNIT, pl.ds(r % UNIT * ROWS, ROWS), :], NT)
            for c, r, _ in pairs
        ]
        terms = []
        for (c, r, weight), value in zip(pairs, cross):
            bias = jnp.concatenate([col[c], col[c]], axis=1) + sq_r[r]
            tile = jnp.exp2(value * GAIN + bias)
            if diagonal:
                row_id = lax.broadcasted_iota(jnp.int32, (ROWS, ROWS), 0)
                col_id = lax.broadcasted_iota(jnp.int32, (ROWS, ROWS), 1)
                tile = jnp.where(row_id == col_id, 0.0, tile)
            term = dot(c_s[c], tile.astype(jnp.bfloat16), NN)
            terms.append(term if diagonal else term * weight)
        for (c, r, _), term in zip(pairs, terms):
            acc[r] = acc[r] + term

    def list_tiles(c_lo, c_hi, r_lo, r_hi):
        def per_c(c, count):
            block_c = idx_ref[1, c]
            for r in range(r_lo, r_hi):
                edges = adj_r[r, block_c] + adj_c[c, idx_ref[0, r]]
                codes[count] = c * 16 + r
                edge_list[count] = edges
                count = count + (edges > 0).astype(jnp.int32)
            return count

        count = lax.fori_loop(c_lo, c_hi, per_c, 0)
        for i in range(GROUPED - 1):
            codes[count + i] = codes[0]
            edge_list[count + i] = 0
        return count

    def run_tiles(count):
        def step(t, carry):
            pairs = []
            for i in range(GROUPED):
                code = codes[t * GROUPED + i]
                pairs.append((code // 16, code % 16, edge_list[t * GROUPED + i].astype(jnp.float32)))
            form(pairs, False)
            return carry

        lax.fori_loop(0, (count + GROUPED - 1) // GROUPED, step, 0)

    if old:
        count = list_tiles(0, old_slots, old_slots, slots)
        for copy in [acc_copy] + r_copies[old:] + c_copies[:old]:
            copy.wait()
        run_tiles(count)
        count = list_tiles(old_slots, slots, 0, slots)
        for copy in c_copies[old:] + r_copies[:old]:
            copy.wait()
        run_tiles(count)
    else:
        acc[...] = jnp.zeros_like(acc)
        count = list_tiles(0, slots, 0, slots)
        for copy in c_copies + r_copies:
            copy.wait()
        form([(s, s, None) for s in range(OWN)], True)
        run_tiles(count)
    if last:
        for out, order in zip(outs, ((0, 1, 2, 3), (4, 5, 8, 9), (10, 11, 6, 7), (12, 13, 14, 15))):
            for k, s in enumerate(order):
                out[k] = acc[s]
    else:
        acc_out[...] = acc[...]


def stage(old, new, index, z_parts, y_parts, acc=None):
    smem = pl.BlockSpec(memory_space=pltpu.SMEM)
    vmem = pl.BlockSpec(memory_space=pltpu.VMEM)
    hbm = pl.BlockSpec(memory_space=pltpu.HBM)
    last = new == UNITS
    operands = [index, *z_parts[:new], *y_parts[:new]]
    in_specs = [smem] + [hbm] * (2 * new)
    if old:
        operands.append(acc)
        in_specs.append(hbm)
    if last:
        out_shape = tuple(jax.ShapeDtypeStruct((OWN, COLS, ROWS), jnp.float32) for _ in range(4))
        out_specs = (vmem,) * 4
    else:
        out_shape = jax.ShapeDtypeStruct((16, COLS, ROWS), jnp.float32)
        out_specs = vmem
    slots = UNIT * new
    return pl.pallas_call(
        functools.partial(stage_kernel, old, new, last),
        out_shape=out_shape,
        in_specs=in_specs,
        out_specs=out_specs,
        scratch_shapes=[
            pltpu.VMEM((new, HALF, FEAT), jnp.bfloat16),
            pltpu.VMEM((new, HALF, FEAT), jnp.bfloat16),
            pltpu.VMEM((slots, COLS, ROWS), jnp.bfloat16),
            pltpu.VMEM((new, SCALED, FEAT), jnp.bfloat16),
            pltpu.VMEM((new, META, FEAT), jnp.bfloat16),
            pltpu.VMEM((new, META, FEAT), jnp.bfloat16),
            pltpu.VMEM((slots, 1, ROWS), jnp.float32),
            pltpu.VMEM((128, ROWS), jnp.float32),
            pltpu.VMEM((slots, ROWS, 128), jnp.float32),
            pltpu.VMEM((2, 16, 128), jnp.int32),
            pltpu.SMEM((16, 128), jnp.int32),
            pltpu.SMEM((16, 128), jnp.int32),
            pltpu.SMEM((264,), jnp.int32),
            pltpu.SMEM((264,), jnp.int32),
            pltpu.VMEM((16, COLS, ROWS), jnp.float32),
            pltpu.SemaphoreType.DMA((new,)),
            pltpu.SemaphoreType.DMA((new,)),
            pltpu.SemaphoreType.DMA((new,)),
            pltpu.SemaphoreType.DMA((new,)),
            pltpu.SemaphoreType.DMA((new,)),
            pltpu.SemaphoreType.DMA((3,)),
        ],
        compiler_params=pltpu.CompilerParams(vmem_limit_bytes=VMEM_LIMIT),
        cost_estimate=pl.CostEstimate(flops=6 * 10**9, bytes_accessed=16 * 2**20, transcendentals=10**6),
        name="stage_%d" % new,
    )(*operands)


def finish_kernel(deg_ref, own_ref, a_ref, b_ref, c_ref, image_ref, gram_ref):
    parts = []
    for b in range(OWN):
        inv = 1.0 / jnp.sqrt(deg_ref[b:b + 1, :])
        parts.append((own_ref[b] + a_ref[b] + (b_ref[b] + c_ref[b])) * inv)
    image = jnp.concatenate(parts, axis=1)
    image_ref[...] = image
    gram_ref[...] = lax.dot_general(
        image, image, NT, precision=lax.Precision.HIGHEST, preferred_element_type=jnp.float32
    )


def finish(degree, own, a, b, c):
    return pl.pallas_call(
        finish_kernel,
        out_shape=(
            jax.ShapeDtypeStruct((COLS, DOCS), jnp.float32),
            jax.ShapeDtypeStruct((COLS, COLS), jnp.float32),
        ),
        compiler_params=pltpu.CompilerParams(vmem_limit_bytes=VMEM_LIMIT),
        name="finish",
    )(degree, own, a, b, c)


def solve_kernel(documents, gram_ref, other_ref, image_ref, out_ref):
    gram = (gram_ref[...] + other_ref[...]) / documents
    row_id = lax.broadcasted_iota(jnp.int32, (COLS, 2 * COLS), 0)
    lane_id = lax.broadcasted_iota(jnp.int32, (COLS, 2 * COLS), 1)
    unit = (row_id[:, :COLS] == lane_id[:, :COLS]).astype(jnp.float32)
    work = jnp.concatenate([gram, unit], axis=1)
    for start in range(0, COLS, PANEL):
        columns = [jnp.broadcast_to(work[:, start + j:start + j + 1], work.shape) for j in range(PANEL)]
        for j in range(PANEL):
            k = start + j
            factor = columns[j] * (1.0 / columns[j][k:k + 1, :])
            factor = jnp.where(row_id > k, factor, 0.0)
            for i in range(j + 1, PANEL):
                columns[i] = columns[i] - factor * columns[j][start + i:start + i + 1, :]
            work = work - factor * work[k:k + 1, :]
    pivots = jnp.sum(jnp.where(row_id == lane_id, work, 0.0), axis=1, keepdims=True)
    inverse = work[:, COLS:] / jnp.sqrt(pivots)
    for b in range(OWN):
        out_ref[b] = lax.dot_general(
            inverse, image_ref[:, b * ROWS:(b + 1) * ROWS], NN,
            precision=lax.Precision.HIGHEST, preferred_element_type=jnp.float32,
        )


def solve(documents, gram, other, image):
    return pl.pallas_call(
        functools.partial(solve_kernel, float(documents)),
        out_shape=jax.ShapeDtypeStruct((OWN, COLS, ROWS), jnp.float32),
        compiler_params=pltpu.CompilerParams(vmem_limit_bytes=SMALL_LIMIT),
        name="solve",
    )(gram, other, image)


def shift_z(k):
    return [(y * SIDE + z, y * SIDE + (z + k) % SIDE) for y in range(SIDE) for z in range(SIDE)]


def shift_y(k):
    return [(y * SIDE + z, (y + k) % SIDE * SIDE + z) for y in range(SIDE) for z in range(SIDE)]


def per_device(embedding, subspace, degree, neighbours, counts):
    position = lax.axis_index("blk")
    y, z = position // SIDE, position % SIDE
    row_ids = jnp.stack([(y * SIDE + (z + k) % SIDE) * OWN + UNIT * h + i for k, h in ARRIVAL for i in range(UNIT)])
    col_ids = jnp.stack([((y + k) % SIDE * SIDE + z) * OWN + UNIT * h + i for k, h in ARRIVAL for i in range(UNIT)])
    index = jnp.stack([row_ids, col_ids]).astype(jnp.int32)

    z_a, z_b, y_a, y_b = prepare(embedding, subspace, degree, neighbours, counts)

    def gather(a, b, shift):
        minus_a = lax.ppermute(a, "blk", shift(1))
        plus_b = lax.ppermute(b, "blk", shift(-1))
        b_next, minus_a = lax.optimization_barrier((b, minus_a))
        a_next, plus_b = lax.optimization_barrier((a, plus_b))
        minus_b = lax.ppermute(b_next, "blk", shift(1))
        plus_a = lax.ppermute(a_next, "blk", shift(-1))
        minus_next, minus_b = lax.optimization_barrier((minus_a, minus_b))
        plus_next, plus_a = lax.optimization_barrier((plus_b, plus_a))
        far_a = lax.ppermute(minus_next, "blk", shift(1))
        far_b = lax.ppermute(plus_next, "blk", shift(-1))
        return a, b, minus_a, plus_b, minus_b, plus_a, far_a, far_b

    z_parts = gather(z_a, z_b, shift_z)
    y_parts = gather(y_a, y_b, shift_y)
    acc = stage(0, 4, index, z_parts, y_parts)
    acc = stage(4, 6, index, z_parts, y_parts, acc)
    own, to_minus, to_plus, to_far = stage(6, 8, index, z_parts, y_parts, acc)
    back_a = lax.ppermute(to_minus, "blk", shift_z(-1))
    back_b = lax.ppermute(to_plus, "blk", shift_z(1))
    back_c = lax.ppermute(to_far, "blk", shift_z(2))
    image, gram = finish(degree, own, back_a, back_b, back_c)

    devices_blk = lax.axis_size("blk")
    devices_dp = lax.axis_size("dp")
    other = lax.ppermute(gram, "dp", [(i, i ^ 1) for i in range(devices_dp)])
    for axis, size, first in (("dp", devices_dp, 2), ("blk", devices_blk, 1)):
        step = first
        while step < size:
            gram = gram + other
            other = lax.ppermute(gram, axis, [(i, i ^ step) for i in range(size)])
            step *= 2
    solved = solve(DOCS * devices_blk * devices_dp, gram, other, image)
    return jnp.swapaxes(solved, 1, 2)


def solution(mesh):
    placed = (
        P(("dp", "blk"), None, None),
        P(("dp", "blk"), None, None),
        P(("dp", "blk"), None),
        P(("dp", "blk"), None),
        P(("dp", "blk")),
    )
    return jax.shard_map(
        per_device,
        mesh=mesh,
        in_specs=placed,
        out_specs=P(("dp", "blk"), None, None),
        check_vma=False,
    )
```

```python
import functools
import math

import jax
import jax.numpy as jnp
from jax import lax
from jax.experimental import pallas as pl
from jax.experimental.pallas import tpu as pltpu
from jax.sharding import PartitionSpec as P

ROWS = 256
FEAT = 1024
COLS = 64
OWN = 4
SIDE = 4
HALF = OWN // 2 * ROWS
DOCS = OWN * ROWS
META = 16
SCALED = 32
UNIT = 2
UNITS = 2 * SIDE
Z_ROWS = META + HALF
Y_X = SCALED + META
Y_ROWS = Y_X + HALF
GROUPED = 4
VMEM_LIMIT = 62 * 2**20
SMALL_LIMIT = 16 * 2**20
PANEL = 8
ARRIVAL = ((0, 0), (0, 1), (-1, 0), (1, 1), (-1, 1), (1, 0), (2, 0), (2, 1))
LOG2E = 1.4426950408889634
GAIN = 2.0 * LOG2E / (4.0 * math.sqrt(FEAT))
BIAS = 2.0 * FEAT * LOG2E / (4.0 * math.sqrt(FEAT))
SQ_GAIN = -LOG2E / (4.0 * math.sqrt(FEAT))

NT = (((1,), (1,)), ((), ()))
NN = (((1,), (0,)), ((), ()))


def dot(a, b, dims):
    return lax.dot_general(a, b, dims, preferred_element_type=jnp.float32)


def prep_kernel(nbr_hbm, cnt_hbm, x_hbm, sub_hbm, deg_hbm, za_ref, zb_ref, ya_ref, yb_ref,
                nbr_ref, cnt_ref, x_ref, sub_ref, deg_ref, small, sems):
    loads = [
        pltpu.make_async_copy(x_hbm.at[pl.ds(b * ROWS, ROWS)], x_ref.at[pl.ds(b * ROWS, ROWS)], sems.at[b])
        for b in range(OWN)
    ]
    extra = [
        pltpu.make_async_copy(nbr_hbm, nbr_ref, sems.at[4]),
        pltpu.make_async_copy(cnt_hbm, cnt_ref, sems.at[5]),
        pltpu.make_async_copy(deg_hbm, deg_ref, sems.at[6]),
        pltpu.make_async_copy(sub_hbm, sub_ref, sems.at[7]),
    ]
    for copy in loads + extra:
        copy.start()
    stores = []

    def store(source, target, which):
        copy = pltpu.make_async_copy(source, target, sems.at[which])
        copy.start()
        stores.append(copy)

    ones = jnp.ones((META, FEAT), jnp.bfloat16)
    squares = []
    for b in range(OWN):
        half, place = b // UNIT, b % UNIT * ROWS
        loads[b].wait()
        source = x_ref.at[pl.ds(b * ROWS, ROWS)]
        store(source, (za_ref, zb_ref)[half].at[pl.ds(META + place, ROWS)], 8 + b)
        store(source, (ya_ref, yb_ref)[half].at[pl.ds(Y_X + place, ROWS)], 12 + b)
        x = x_ref[b * ROWS:(b + 1) * ROWS, :].astype(jnp.float32)
        sq = x * x
        high = sq.astype(jnp.bfloat16)
        low = (sq - high.astype(jnp.float32)).astype(jnp.bfloat16)
        squares.append(dot(ones, high, NT) + dot(ones, low, NT))
    for copy in extra:
        copy.wait()
    lane = lax.broadcasted_iota(jnp.int32, (1, 128), 1)
    which = lax.broadcasted_iota(jnp.int32, (META, FEAT), 0)
    pad = jnp.zeros((1, FEAT - 128), jnp.float32)
    for half in range(2):
        total = jnp.concatenate(squares[half * UNIT:(half + 1) * UNIT] + [jnp.zeros((META, FEAT - HALF), jnp.float32)], axis=1)
        s_high = total.astype(jnp.bfloat16).astype(jnp.float32)
        rest = total - s_high
        s_mid = rest.astype(jnp.bfloat16).astype(jnp.float32)
        s_low = rest - s_mid
        meta = jnp.where(which == 0, s_high, jnp.where(which == 1, s_mid, jnp.where(which == 2, s_low, 0.0)))
        for i in range(UNIT):
            b = half * UNIT + i
            row = jnp.zeros((1, 128), jnp.float32)
            for k in range(nbr_ref.shape[1]):
                used = (k < cnt_ref[b]).astype(jnp.float32)
                row = row + jnp.where(lane == nbr_ref[b, k], used, 0.0)
            meta = jnp.where(which == 4 + i, jnp.concatenate([row, pad], axis=1), meta)
            inv = 1.0 / jnp.sqrt(deg_ref[b:b + 1, :])
            scaled = (sub_ref[b] * inv).astype(jnp.bfloat16)
            small[half, 16 * i:16 * (i + 1), :] = jnp.concatenate(
                [scaled[16 * g:16 * (g + 1), :] for g in range(4)], axis=1
            )
        small[half, SCALED:Y_X, :] = meta.astype(jnp.bfloat16)
        store(small.at[half], (ya_ref, yb_ref)[half].at[pl.ds(0, Y_X)], 16 + half)
        store(small.at[half, pl.ds(SCALED, META)], (za_ref, zb_ref)[half].at[pl.ds(0, META)], 18 + half)
    for copy in stores:
        copy.wait()


def prepare(embedding, subspace, degree, neighbours, counts):
    hbm = pl.BlockSpec(memory_space=pltpu.HBM)
    return pl.pallas_call(
        prep_kernel,
        out_shape=(jax.ShapeDtypeStruct((Z_ROWS, FEAT), jnp.bfloat16),) * 2
        + (jax.ShapeDtypeStruct((Y_ROWS, FEAT), jnp.bfloat16),) * 2,
        in_specs=[hbm] * 5,
        out_specs=(hbm,) * 4,
        scratch_shapes=[
            pltpu.SMEM(neighbours.shape, jnp.int32),
            pltpu.SMEM(counts.shape, jnp.int32),
            pltpu.VMEM((DOCS, FEAT), jnp.bfloat16),
            pltpu.VMEM((OWN, COLS, ROWS), jnp.float32),
            pltpu.VMEM((OWN, ROWS), jnp.float32),
            pltpu.VMEM((2, Y_X, FEAT), jnp.bfloat16),
            pltpu.SemaphoreType.DMA((20,)),
        ],
        compiler_params=pltpu.CompilerParams(vmem_limit_bytes=VMEM_LIMIT),
        name="prepare",
    )(neighbours, counts, embedding.reshape(DOCS, FEAT), jnp.swapaxes(subspace, 1, 2), degree)


def stage_kernel(old, new, last, *refs):
    idx_ref = refs[0]
    z_refs = refs[1:1 + new]
    y_refs = refs[1 + new:1 + 2 * new]
    rest = refs[1 + 2 * new:]
    if old:
        acc_in, rest = rest[0], rest[1:]
    if last:
        outs, rest = rest[:4], rest[4:]
    else:
        acc_out, rest = rest[0], rest[1:]
    (r_x, c_x, c_s, c_pack, meta_r, meta_c, sq_r, sq_c, col, adj_vmem, adj_r, adj_c, codes, edge_list, acc,
     sem_r, sem_c, sem_s, sem_m, sem_n, sem_a) = rest
    old_slots, slots = UNIT * old, UNIT * new

    meta_copies = []
    pack_copies = []
    r_copies = []
    c_copies = []
    for u in range(new):
        meta_copies.append(pltpu.make_async_copy(z_refs[u].at[pl.ds(0, META)], meta_r.at[u], sem_m.at[u]))
        meta_copies.append(pltpu.make_async_copy(y_refs[u].at[pl.ds(SCALED, META)], meta_c.at[u], sem_n.at[u]))
        pack_copies.append(pltpu.make_async_copy(y_refs[u].at[pl.ds(0, SCALED)], c_pack.at[u], sem_s.at[u]))
        r_copies.append(pltpu.make_async_copy(z_refs[u].at[pl.ds(META, HALF)], r_x.at[u], sem_r.at[u]))
        c_copies.append(pltpu.make_async_copy(y_refs[u].at[pl.ds(Y_X, HALF)], c_x.at[u], sem_c.at[u]))
    if old:
        acc_copy = pltpu.make_async_copy(acc_in, acc, sem_a.at[2])
    for copy in meta_copies:
        copy.start()
    for copy in r_copies[old:] + c_copies[:old] + pack_copies:
        copy.start()
    if old:
        acc_copy.start()
    for copy in c_copies[old:] + r_copies[:old]:
        copy.start()

    for copy in meta_copies:
        copy.wait()
    for side, (meta, keep, adj) in enumerate(((meta_r, sq_r, adj_r), (meta_c, sq_c, adj_c))):
        for u in range(new):
            m = meta[u].astype(jnp.float32)
            total = (m[0:1, 0:HALF] + m[1:2, 0:HALF] + m[2:3, 0:HALF]) * SQ_GAIN
            for i in range(UNIT):
                piece = total[:, i * ROWS:(i + 1) * ROWS]
                if side == 0:
                    keep[u * UNIT + i] = piece + BIAS
                else:
                    keep[u * UNIT + i:u * UNIT + i + 1, :] = piece
            adj_vmem[side, u * UNIT:(u + 1) * UNIT, :] = m[4:4 + UNIT, 0:128].astype(jnp.int32)
        pltpu.make_async_copy(adj_vmem.at[side], adj, sem_a.at[side]).start()
    columns = jnp.transpose(sq_c[...])
    for s in range(slots):
        col[s] = jnp.broadcast_to(columns[:, s:s + 1], (ROWS, 128))
    for copy in pack_copies:
        copy.wait()
    for s in range(slots):
        p = c_pack[s // UNIT, 16 * (s % UNIT):16 * (s % UNIT + 1), :]
        c_s[s] = jnp.concatenate([p[:, ROWS * k:ROWS * (k + 1)] for k in range(4)], axis=0)
    for side, adj in enumerate((adj_r, adj_c)):
        pltpu.make_async_copy(adj_vmem.at[side], adj, sem_a.at[side]).wait()

    def form(pairs, diagonal):
        cross = [
            dot(c_x[c // UNIT, pl.ds(c % UNIT * ROWS, ROWS), :], r_x[r // UNIT, pl.ds(r % UNIT * ROWS, ROWS), :], NT)
            for c, r, _ in pairs
        ]
        terms = []
        for (c, r, weight), value in zip(pairs, cross):
            bias = jnp.concatenate([col[c], col[c]], axis=1) + sq_r[r]
            tile = jnp.exp2(value * GAIN + bias)
            if diagonal:
                row_id = lax.broadcasted_iota(jnp.int32, (ROWS, ROWS), 0)
                col_id = lax.broadcasted_iota(jnp.int32, (ROWS, ROWS), 1)
                tile = jnp.where(row_id == col_id, 0.0, tile)
            term = dot(c_s[c], tile.astype(jnp.bfloat16), NN)
            terms.append(term if diagonal else term * weight)
        for (c, r, _), term in zip(pairs, terms):
            acc[r] = acc[r] + term

    def list_tiles(c_lo, c_hi, r_lo, r_hi):
        def per_c(c, count):
            block_c = idx_ref[1, c]
            for r in range(r_lo, r_hi):
                edges = adj_r[r, block_c] + adj_c[c, idx_ref[0, r]]
                codes[count] = c * 16 + r
                edge_list[count] = edges
                count = count + (edges > 0).astype(jnp.int32)
            return count

        count = lax.fori_loop(c_lo, c_hi, per_c, 0)
        for i in range(GROUPED - 1):
            codes[count + i] = codes[0]
            edge_list[count + i] = 0
        return count

    def run_tiles(count):
        def step(t, carry):
            pairs = []
            for i in range(GROUPED):
                code = codes[t * GROUPED + i]
                pairs.append((code // 16, code % 16, edge_list[t * GROUPED + i].astype(jnp.float32)))
            form(pairs, False)
            return carry

        lax.fori_loop(0, (count + GROUPED - 1) // GROUPED, step, 0)

    if old:
        count = list_tiles(0, old_slots, old_slots, slots)
        for copy in [acc_copy] + r_copies[old:] + c_copies[:old]:
            copy.wait()
        run_tiles(count)
        count = list_tiles(old_slots, slots, 0, slots)
        for copy in c_copies[old:] + r_copies[:old]:
            copy.wait()
        run_tiles(count)
    else:
        acc[...] = jnp.zeros_like(acc)
        count = list_tiles(0, slots, 0, slots)
        for copy in c_copies + r_copies:
            copy.wait()
        form([(s, s, None) for s in range(OWN)], True)
        run_tiles(count)
    if last:
        for out, order in zip(outs, ((0, 1, 2, 3), (4, 5, 8, 9), (10, 11, 6, 7), (12, 13, 14, 15))):
            for k, s in enumerate(order):
                out[k] = acc[s].astype(out.dtype)
    else:
        acc_out[...] = acc[...]


def stage(old, new, index, z_parts, y_parts, acc=None):
    smem = pl.BlockSpec(memory_space=pltpu.SMEM)
    vmem = pl.BlockSpec(memory_space=pltpu.VMEM)
    hbm = pl.BlockSpec(memory_space=pltpu.HBM)
    last = new == UNITS
    operands = [index, *z_parts[:new], *y_parts[:new]]
    in_specs = [smem] + [hbm] * (2 * new)
    if old:
        operands.append(acc)
        in_specs.append(hbm)
    if last:
        out_shape = tuple(
            jax.ShapeDtypeStruct((OWN, COLS, ROWS), kind) for kind in (jnp.float32,) * 4
        )
        out_specs = (vmem,) * 4
    else:
        out_shape = jax.ShapeDtypeStruct((16, COLS, ROWS), jnp.float32)
        out_specs = vmem
    slots = UNIT * new
    return pl.pallas_call(
        functools.partial(stage_kernel, old, new, last),
        out_shape=out_shape,
        in_specs=in_specs,
        out_specs=out_specs,
        scratch_shapes=[
            pltpu.VMEM((new, HALF, FEAT), jnp.bfloat16),
            pltpu.VMEM((new, HALF, FEAT), jnp.bfloat16),
            pltpu.VMEM((slots, COLS, ROWS), jnp.bfloat16),
            pltpu.VMEM((new, SCALED, FEAT), jnp.bfloat16),
            pltpu.VMEM((new, META, FEAT), jnp.bfloat16),
            pltpu.VMEM((new, META, FEAT), jnp.bfloat16),
            pltpu.VMEM((slots, 1, ROWS), jnp.float32),
            pltpu.VMEM((128, ROWS), jnp.float32),
            pltpu.VMEM((slots, ROWS, 128), jnp.float32),
            pltpu.VMEM((2, 16, 128), jnp.int32),
            pltpu.SMEM((16, 128), jnp.int32),
            pltpu.SMEM((16, 128), jnp.int32),
            pltpu.SMEM((264,), jnp.int32),
            pltpu.SMEM((264,), jnp.int32),
            pltpu.VMEM((16, COLS, ROWS), jnp.float32),
            pltpu.SemaphoreType.DMA((new,)),
            pltpu.SemaphoreType.DMA((new,)),
            pltpu.SemaphoreType.DMA((new,)),
            pltpu.SemaphoreType.DMA((new,)),
            pltpu.SemaphoreType.DMA((new,)),
            pltpu.SemaphoreType.DMA((3,)),
        ],
        compiler_params=pltpu.CompilerParams(vmem_limit_bytes=VMEM_LIMIT),
        cost_estimate=pl.CostEstimate(flops=6 * 10**9, bytes_accessed=16 * 2**20, transcendentals=10**6),
        name="stage_%d" % new,
    )(*operands)


def finish_kernel(deg_ref, own_ref, a_ref, b_ref, c_ref, image_ref, gram_ref):
    parts = []
    for b in range(OWN):
        inv = 1.0 / jnp.sqrt(deg_ref[b:b + 1, :])
        far = [ref[b].astype(jnp.float32) for ref in (a_ref, b_ref, c_ref)]
        parts.append((own_ref[b] + far[0] + (far[1] + far[2])) * inv)
    image = jnp.concatenate(parts, axis=1)
    image_ref[...] = image
    gram = lax.dot_general(
        image, image, NT, precision=lax.Precision.HIGHEST, preferred_element_type=jnp.float32
    )
    gram_ref[...] = jnp.concatenate([gram[:COLS // 2], gram[COLS // 2:]], axis=1)


def finish(degree, own, a, b, c):
    return pl.pallas_call(
        finish_kernel,
        out_shape=(
            jax.ShapeDtypeStruct((COLS, DOCS), jnp.float32),
            jax.ShapeDtypeStruct((COLS // 2, 2 * COLS), jnp.float32),
        ),
        compiler_params=pltpu.CompilerParams(vmem_limit_bytes=SMALL_LIMIT),
        name="finish",
    )(degree, own, a, b, c)


def solve_kernel(documents, gram_ref, other_ref, image_hbm, out_ref, image_ref, sem):
    load = pltpu.make_async_copy(image_hbm, image_ref, sem)
    load.start()
    packed = (gram_ref[...] + other_ref[...]) / documents
    gram = jnp.concatenate([packed[:, :COLS], packed[:, COLS:]], axis=0)
    row_id = lax.broadcasted_iota(jnp.int32, (COLS, 2 * COLS), 0)
    lane_id = lax.broadcasted_iota(jnp.int32, (COLS, 2 * COLS), 1)
    unit = (row_id[:, :COLS] == lane_id[:, :COLS]).astype(jnp.float32)
    work = jnp.concatenate([gram, unit], axis=1)
    for start in range(0, COLS, PANEL):
        columns = [jnp.broadcast_to(work[:, start + j:start + j + 1], work.shape) for j in range(PANEL)]
        for j in range(PANEL):
            k = start + j
            factor = columns[j] * (1.0 / columns[j][k:k + 1, :])
            factor = jnp.where(row_id > k, factor, 0.0)
            for i in range(j + 1, PANEL):
                columns[i] = columns[i] - factor * columns[j][start + i:start + i + 1, :]
            work = work - factor * work[k:k + 1, :]
    pivots = jnp.sum(jnp.where(row_id == lane_id, work, 0.0), axis=1, keepdims=True)
    inverse = work[:, COLS:] / jnp.sqrt(pivots)
    load.wait()
    for b in range(OWN):
        out_ref[b] = lax.dot_general(
            inverse, image_ref[:, b * ROWS:(b + 1) * ROWS], NN,
            precision=lax.Precision.HIGHEST, preferred_element_type=jnp.float32,
        )


def solve(documents, gram, other, image):
    vmem = pl.BlockSpec(memory_space=pltpu.VMEM)
    return pl.pallas_call(
        functools.partial(solve_kernel, float(documents)),
        out_shape=jax.ShapeDtypeStruct((OWN, COLS, ROWS), jnp.float32),
        in_specs=[vmem, vmem, pl.BlockSpec(memory_space=pltpu.HBM)],
        scratch_shapes=[pltpu.VMEM((COLS, DOCS), jnp.float32), pltpu.SemaphoreType.DMA],
        compiler_params=pltpu.CompilerParams(vmem_limit_bytes=SMALL_LIMIT),
        name="solve",
    )(gram, other, image)


def shift_z(k):
    return [(y * SIDE + z, y * SIDE + (z + k) % SIDE) for y in range(SIDE) for z in range(SIDE)]


def shift_y(k):
    return [(y * SIDE + z, (y + k) % SIDE * SIDE + z) for y in range(SIDE) for z in range(SIDE)]


def per_device(embedding, subspace, degree, neighbours, counts):
    position = lax.axis_index("blk")
    y, z = position // SIDE, position % SIDE
    row_ids = jnp.stack([(y * SIDE + (z + k) % SIDE) * OWN + UNIT * h + i for k, h in ARRIVAL for i in range(UNIT)])
    col_ids = jnp.stack([((y + k) % SIDE * SIDE + z) * OWN + UNIT * h + i for k, h in ARRIVAL for i in range(UNIT)])
    index = jnp.stack([row_ids, col_ids]).astype(jnp.int32)

    z_a, z_b, y_a, y_b = prepare(embedding, subspace, degree, neighbours, counts)

    def gather(a, b, shift):
        minus_a = lax.ppermute(a, "blk", shift(1))
        plus_b = lax.ppermute(b, "blk", shift(-1))
        b_next, minus_a = lax.optimization_barrier((b, minus_a))
        a_next, plus_b = lax.optimization_barrier((a, plus_b))
        minus_b = lax.ppermute(b_next, "blk", shift(1))
        plus_a = lax.ppermute(a_next, "blk", shift(-1))
        minus_next, minus_b = lax.optimization_barrier((minus_a, minus_b))
        plus_next, plus_a = lax.optimization_barrier((plus_b, plus_a))
        far_a = lax.ppermute(minus_next, "blk", shift(1))
        far_b = lax.ppermute(plus_next, "blk", shift(-1))
        return a, b, minus_a, plus_b, minus_b, plus_a, far_a, far_b

    z_parts = gather(z_a, z_b, shift_z)
    y_parts = gather(y_a, y_b, shift_y)
    acc = stage(0, 4, index, z_parts, y_parts)
    acc = stage(4, 6, index, z_parts, y_parts, acc)
    own, to_minus, to_plus, to_far = stage(6, 8, index, z_parts, y_parts, acc)
    back_a = lax.ppermute(to_minus, "blk", shift_z(-1))
    back_b = lax.ppermute(to_plus, "blk", shift_z(1))
    back_c = lax.ppermute(to_far, "blk", shift_z(2))
    image, gram = finish(degree, own, back_a, back_b, back_c)

    devices_blk = lax.axis_size("blk")
    devices_dp = lax.axis_size("dp")
    other = lax.ppermute(gram, "dp", [(i, i ^ 1) for i in range(devices_dp)])
    for axis, size, first in (("dp", devices_dp, 2), ("blk", devices_blk, 1)):
        step = first
        while step < size:
            gram = gram + other
            other = lax.ppermute(gram, axis, [(i, i ^ step) for i in range(size)])
            step *= 2
    solved = solve(DOCS * devices_blk * devices_dp, gram, other, image)
    return jnp.swapaxes(solved, 1, 2)


def solution(mesh):
    placed = (
        P(("dp", "blk"), None, None),
        P(("dp", "blk"), None, None),
        P(("dp", "blk"), None),
        P(("dp", "blk"), None),
        P(("dp", "blk")),
    )
    return jax.shard_map(
        per_device,
        mesh=mesh,
        in_specs=placed,
        out_specs=P(("dp", "blk"), None, None),
        check_vma=False,
    )
```

```python
import functools
import math

import jax
import jax.numpy as jnp
from jax import lax
from jax.experimental import pallas as pl
from jax.experimental.pallas import tpu as pltpu
from jax.sharding import PartitionSpec as P

ROWS = 256
FEAT = 1024
COLS = 64
OWN = 4
SIDE = 4
HALF = OWN // 2 * ROWS
DOCS = OWN * ROWS
META = 16
SCALED = 32
UNIT = 2
UNITS = 2 * SIDE
Z_ROWS = META + HALF
Y_X = SCALED + META
Y_ROWS = Y_X + HALF
GROUPED = 8
VMEM_LIMIT = 62 * 2**20
SMALL_LIMIT = 16 * 2**20
PANEL = 8
ARRIVAL = ((0, 0), (0, 1), (-1, 0), (1, 1), (-1, 1), (1, 0), (2, 0), (2, 1))
LOG2E = 1.4426950408889634
GAIN = 2.0 * LOG2E / (4.0 * math.sqrt(FEAT))
BIAS = 2.0 * FEAT * LOG2E / (4.0 * math.sqrt(FEAT))
SQ_GAIN = -LOG2E / (4.0 * math.sqrt(FEAT))

NT = (((1,), (1,)), ((), ()))
NN = (((1,), (0,)), ((), ()))


def dot(a, b, dims):
    return lax.dot_general(a, b, dims, preferred_element_type=jnp.float32)


def prep_kernel(nbr_hbm, cnt_hbm, x_hbm, sub_hbm, deg_hbm, za_ref, zb_ref, ya_ref, yb_ref,
                nbr_ref, cnt_ref, x_ref, sub_ref, deg_ref, small, sems):
    loads = [
        pltpu.make_async_copy(x_hbm.at[pl.ds(b * ROWS, ROWS)], x_ref.at[pl.ds(b * ROWS, ROWS)], sems.at[b])
        for b in range(OWN)
    ]
    extra = [
        pltpu.make_async_copy(nbr_hbm, nbr_ref, sems.at[4]),
        pltpu.make_async_copy(cnt_hbm, cnt_ref, sems.at[5]),
        pltpu.make_async_copy(deg_hbm, deg_ref, sems.at[6]),
        pltpu.make_async_copy(sub_hbm, sub_ref, sems.at[7]),
    ]
    for copy in loads + extra:
        copy.start()
    stores = []

    def store(source, target, which):
        copy = pltpu.make_async_copy(source, target, sems.at[which])
        copy.start()
        stores.append(copy)

    ones = jnp.ones((META, FEAT), jnp.bfloat16)
    squares = []
    for b in range(OWN):
        half, place = b // UNIT, b % UNIT * ROWS
        loads[b].wait()
        source = x_ref.at[pl.ds(b * ROWS, ROWS)]
        store(source, (za_ref, zb_ref)[half].at[pl.ds(META + place, ROWS)], 8 + b)
        store(source, (ya_ref, yb_ref)[half].at[pl.ds(Y_X + place, ROWS)], 12 + b)
        x = x_ref[b * ROWS:(b + 1) * ROWS, :].astype(jnp.float32)
        sq = x * x
        high = sq.astype(jnp.bfloat16)
        low = (sq - high.astype(jnp.float32)).astype(jnp.bfloat16)
        squares.append(dot(ones, high, NT) + dot(ones, low, NT))
    for copy in extra:
        copy.wait()
    lane = lax.broadcasted_iota(jnp.int32, (1, 128), 1)
    which = lax.broadcasted_iota(jnp.int32, (META, FEAT), 0)
    pad = jnp.zeros((1, FEAT - 128), jnp.float32)
    for half in range(2):
        total = jnp.concatenate(squares[half * UNIT:(half + 1) * UNIT] + [jnp.zeros((META, FEAT - HALF), jnp.float32)], axis=1)
        s_high = total.astype(jnp.bfloat16).astype(jnp.float32)
        rest = total - s_high
        s_mid = rest.astype(jnp.bfloat16).astype(jnp.float32)
        s_low = rest - s_mid
        meta = jnp.where(which == 0, s_high, jnp.where(which == 1, s_mid, jnp.where(which == 2, s_low, 0.0)))
        for i in range(UNIT):
            b = half * UNIT + i
            row = jnp.zeros((1, 128), jnp.float32)
            for k in range(nbr_ref.shape[1]):
                used = (k < cnt_ref[b]).astype(jnp.float32)
                row = row + jnp.where(lane == nbr_ref[b, k], used, 0.0)
            meta = jnp.where(which == 4 + i, jnp.concatenate([row, pad], axis=1), meta)
            inv = 1.0 / jnp.sqrt(deg_ref[b:b + 1, :])
            scaled = (sub_ref[b] * inv).astype(jnp.bfloat16)
            small[half, 16 * i:16 * (i + 1), :] = jnp.concatenate(
                [scaled[16 * g:16 * (g + 1), :] for g in range(4)], axis=1
            )
        small[half, SCALED:Y_X, :] = meta.astype(jnp.bfloat16)
        store(small.at[half], (ya_ref, yb_ref)[half].at[pl.ds(0, Y_X)], 16 + half)
        store(small.at[half, pl.ds(SCALED, META)], (za_ref, zb_ref)[half].at[pl.ds(0, META)], 18 + half)
    for copy in stores:
        copy.wait()


def prepare(embedding, subspace, degree, neighbours, counts):
    hbm = pl.BlockSpec(memory_space=pltpu.HBM)
    return pl.pallas_call(
        prep_kernel,
        out_shape=(jax.ShapeDtypeStruct((Z_ROWS, FEAT), jnp.bfloat16),) * 2
        + (jax.ShapeDtypeStruct((Y_ROWS, FEAT), jnp.bfloat16),) * 2,
        in_specs=[hbm] * 5,
        out_specs=(hbm,) * 4,
        scratch_shapes=[
            pltpu.SMEM(neighbours.shape, jnp.int32),
            pltpu.SMEM(counts.shape, jnp.int32),
            pltpu.VMEM((DOCS, FEAT), jnp.bfloat16),
            pltpu.VMEM((OWN, COLS, ROWS), jnp.float32),
            pltpu.VMEM((OWN, ROWS), jnp.float32),
            pltpu.VMEM((2, Y_X, FEAT), jnp.bfloat16),
            pltpu.SemaphoreType.DMA((20,)),
        ],
        compiler_params=pltpu.CompilerParams(vmem_limit_bytes=VMEM_LIMIT),
        name="prepare",
    )(neighbours, counts, embedding.reshape(DOCS, FEAT), jnp.swapaxes(subspace, 1, 2), degree)


def stage_kernel(old, new, last, *refs):
    idx_ref = refs[0]
    z_refs = refs[1:1 + new]
    y_refs = refs[1 + new:1 + 2 * new]
    rest = refs[1 + 2 * new:]
    if old:
        acc_in, rest = rest[0], rest[1:]
    if last:
        outs, rest = rest[:4], rest[4:]
    else:
        acc_out, rest = rest[0], rest[1:]
    (r_x, c_x, c_s, c_pack, meta_r, meta_c, sq_r, sq_c, col, adj_vmem, adj_r, adj_c, codes, edge_list, acc,
     sem_r, sem_c, sem_s, sem_m, sem_n, sem_a) = rest
    old_slots, slots = UNIT * old, UNIT * new

    meta_copies = []
    pack_copies = []
    r_copies = []
    c_copies = []
    for u in range(new):
        meta_copies.append(pltpu.make_async_copy(z_refs[u].at[pl.ds(0, META)], meta_r.at[u], sem_m.at[u]))
        meta_copies.append(pltpu.make_async_copy(y_refs[u].at[pl.ds(SCALED, META)], meta_c.at[u], sem_n.at[u]))
        pack_copies.append(pltpu.make_async_copy(y_refs[u].at[pl.ds(0, SCALED)], c_pack.at[u], sem_s.at[u]))
        r_copies.append(pltpu.make_async_copy(z_refs[u].at[pl.ds(META, HALF)], r_x.at[u], sem_r.at[u]))
        c_copies.append(pltpu.make_async_copy(y_refs[u].at[pl.ds(Y_X, HALF)], c_x.at[u], sem_c.at[u]))
    if old:
        acc_copy = pltpu.make_async_copy(acc_in, acc, sem_a.at[2])
    if old:
        sweeps = [
            ((0, old_slots, old_slots, slots), r_copies[old:] + c_copies[:old]),
            ((old_slots, slots, 0, slots), c_copies[old:] + r_copies[:old]),
        ]
    else:
        sweeps = [((0, slots, 0, slots), c_copies + r_copies)]
    for copy in meta_copies:
        copy.start()
    for copy in sweeps[0][1] + pack_copies:
        copy.start()
    if old:
        acc_copy.start()

    for copy in meta_copies:
        copy.wait()
    for side, (meta, keep, adj) in enumerate(((meta_r, sq_r, adj_r), (meta_c, sq_c, adj_c))):
        for u in range(new):
            m = meta[u].astype(jnp.float32)
            total = (m[0:1, 0:HALF] + m[1:2, 0:HALF] + m[2:3, 0:HALF]) * SQ_GAIN
            for i in range(UNIT):
                piece = total[:, i * ROWS:(i + 1) * ROWS]
                if side == 0:
                    keep[u * UNIT + i] = piece + BIAS
                else:
                    keep[u * UNIT + i:u * UNIT + i + 1, :] = piece
            adj_vmem[side, u * UNIT:(u + 1) * UNIT, :] = m[4:4 + UNIT, 0:128].astype(jnp.int32)
        pltpu.make_async_copy(adj_vmem.at[side], adj, sem_a.at[side]).start()
    columns = jnp.transpose(sq_c[...])
    for s in range(slots):
        col[s] = jnp.broadcast_to(columns[:, s:s + 1], (ROWS, 128))
    for copy in pack_copies:
        copy.wait()
    for s in range(slots):
        p = c_pack[s // UNIT, 16 * (s % UNIT):16 * (s % UNIT + 1), :]
        c_s[s] = jnp.concatenate([p[:, ROWS * k:ROWS * (k + 1)] for k in range(4)], axis=0)
    for side, adj in enumerate((adj_r, adj_c)):
        pltpu.make_async_copy(adj_vmem.at[side], adj, sem_a.at[side]).wait()

    def form(pairs, diagonal):
        cross = [
            dot(c_x[c // UNIT, pl.ds(c % UNIT * ROWS, ROWS), :], r_x[r // UNIT, pl.ds(r % UNIT * ROWS, ROWS), :], NT)
            for c, r, _ in pairs
        ]
        terms = []
        for (c, r, weight), value in zip(pairs, cross):
            bias = jnp.concatenate([col[c], col[c]], axis=1) + sq_r[r]
            tile = jnp.exp2(value * GAIN + bias)
            if diagonal:
                row_id = lax.broadcasted_iota(jnp.int32, (ROWS, ROWS), 0)
                col_id = lax.broadcasted_iota(jnp.int32, (ROWS, ROWS), 1)
                tile = jnp.where(row_id == col_id, 0.0, tile)
            term = dot(c_s[c], tile.astype(jnp.bfloat16), NN)
            terms.append(term if diagonal else term * weight)
        for (c, r, _), term in zip(pairs, terms):
            acc[r] = acc[r] + term

    def list_tiles(c_lo, c_hi, r_lo, r_hi):
        def per_c(c, count):
            block_c = idx_ref[1, c]
            for r in range(r_lo, r_hi):
                edges = adj_r[r, block_c] + adj_c[c, idx_ref[0, r]]
                codes[count] = c * 16 + r
                edge_list[count] = edges
                count = count + (edges > 0).astype(jnp.int32)
            return count

        count = lax.fori_loop(c_lo, c_hi, per_c, 0)
        for i in range(GROUPED - 1):
            codes[count + i] = codes[0]
            edge_list[count + i] = 0
        return count

    def run_tiles(count):
        def step(t, carry):
            pairs = []
            for i in range(GROUPED):
                code = codes[t * GROUPED + i]
                pairs.append((code // 16, code % 16, edge_list[t * GROUPED + i].astype(jnp.float32)))
            form(pairs, False)
            return carry

        lax.fori_loop(0, (count + GROUPED - 1) // GROUPED, step, 0)

    if old:
        acc_copy.wait()
    else:
        acc[...] = jnp.zeros_like(acc)
    for which, (span, loads) in enumerate(sweeps):
        count = list_tiles(*span)
        for copy in loads:
            copy.wait()
        if which + 1 < len(sweeps):
            for copy in sweeps[which + 1][1]:
                copy.start()
        if not old:
            form([(s, s, None) for s in range(OWN)], True)
        run_tiles(count)
    if last:
        for out, order in zip(outs, ((0, 1, 2, 3), (4, 5, 8, 9), (10, 11, 6, 7), (12, 13, 14, 15))):
            for k, s in enumerate(order):
                out[k] = acc[s].astype(out.dtype)
    else:
        acc_out[...] = acc[...]


def stage(old, new, index, z_parts, y_parts, acc=None):
    smem = pl.BlockSpec(memory_space=pltpu.SMEM)
    vmem = pl.BlockSpec(memory_space=pltpu.VMEM)
    hbm = pl.BlockSpec(memory_space=pltpu.HBM)
    last = new == UNITS
    operands = [index, *z_parts[:new], *y_parts[:new]]
    in_specs = [smem] + [hbm] * (2 * new)
    if old:
        operands.append(acc)
        in_specs.append(hbm)
    if last:
        out_shape = tuple(
            jax.ShapeDtypeStruct((OWN, COLS, ROWS), kind) for kind in (jnp.float32,) * 4
        )
        out_specs = (vmem,) * 4
    else:
        out_shape = jax.ShapeDtypeStruct((16, COLS, ROWS), jnp.float32)
        out_specs = vmem
    slots = UNIT * new
    return pl.pallas_call(
        functools.partial(stage_kernel, old, new, last),
        out_shape=out_shape,
        in_specs=in_specs,
        out_specs=out_specs,
        scratch_shapes=[
            pltpu.VMEM((new, HALF, FEAT), jnp.bfloat16),
            pltpu.VMEM((new, HALF, FEAT), jnp.bfloat16),
            pltpu.VMEM((slots, COLS, ROWS), jnp.bfloat16),
            pltpu.VMEM((new, SCALED, FEAT), jnp.bfloat16),
            pltpu.VMEM((new, META, FEAT), jnp.bfloat16),
            pltpu.VMEM((new, META, FEAT), jnp.bfloat16),
            pltpu.VMEM((slots, 1, ROWS), jnp.float32),
            pltpu.VMEM((128, ROWS), jnp.float32),
            pltpu.VMEM((slots, ROWS, 128), jnp.float32),
            pltpu.VMEM((2, 16, 128), jnp.int32),
            pltpu.SMEM((16, 128), jnp.int32),
            pltpu.SMEM((16, 128), jnp.int32),
            pltpu.SMEM((264,), jnp.int32),
            pltpu.SMEM((264,), jnp.int32),
            pltpu.VMEM((16, COLS, ROWS), jnp.float32),
            pltpu.SemaphoreType.DMA((new,)),
            pltpu.SemaphoreType.DMA((new,)),
            pltpu.SemaphoreType.DMA((new,)),
            pltpu.SemaphoreType.DMA((new,)),
            pltpu.SemaphoreType.DMA((new,)),
            pltpu.SemaphoreType.DMA((3,)),
        ],
        compiler_params=pltpu.CompilerParams(vmem_limit_bytes=VMEM_LIMIT),
        cost_estimate=pl.CostEstimate(flops=6 * 10**9, bytes_accessed=16 * 2**20, transcendentals=10**6),
        name="stage_%d" % new,
    )(*operands)


def finish_kernel(deg_ref, own_ref, a_ref, b_ref, c_ref, image_ref, gram_ref):
    parts = []
    for b in range(OWN):
        inv = 1.0 / jnp.sqrt(deg_ref[b:b + 1, :])
        far = [ref[b].astype(jnp.float32) for ref in (a_ref, b_ref, c_ref)]
        parts.append((own_ref[b] + far[0] + (far[1] + far[2])) * inv)
    image = jnp.concatenate(parts, axis=1)
    image_ref[...] = image
    gram = lax.dot_general(
        image, image, NT, precision=lax.Precision.HIGHEST, preferred_element_type=jnp.float32
    )
    gram_ref[...] = jnp.concatenate([gram[:COLS // 2], gram[COLS // 2:]], axis=1)


def finish(degree, own, a, b, c):
    return pl.pallas_call(
        finish_kernel,
        out_shape=(
            jax.ShapeDtypeStruct((COLS, DOCS), jnp.float32),
            jax.ShapeDtypeStruct((COLS // 2, 2 * COLS), jnp.float32),
        ),
        compiler_params=pltpu.CompilerParams(vmem_limit_bytes=SMALL_LIMIT),
        name="finish",
    )(degree, own, a, b, c)


def solve_kernel(documents, gram_ref, other_ref, image_hbm, out_ref, image_ref, sem):
    load = pltpu.make_async_copy(image_hbm, image_ref, sem)
    load.start()
    packed = (gram_ref[...] + other_ref[...]) / documents
    gram = jnp.concatenate([packed[:, :COLS], packed[:, COLS:]], axis=0)
    row_id = lax.broadcasted_iota(jnp.int32, (COLS, 2 * COLS), 0)
    lane_id = lax.broadcasted_iota(jnp.int32, (COLS, 2 * COLS), 1)
    unit = (row_id[:, :COLS] == lane_id[:, :COLS]).astype(jnp.float32)
    work = jnp.concatenate([gram, unit], axis=1)
    for start in range(0, COLS, PANEL):
        columns = [jnp.broadcast_to(work[:, start + j:start + j + 1], work.shape) for j in range(PANEL)]
        for j in range(PANEL):
            k = start + j
            factor = columns[j] * (1.0 / columns[j][k:k + 1, :])
            factor = jnp.where(row_id > k, factor, 0.0)
            for i in range(j + 1, PANEL):
                columns[i] = columns[i] - factor * columns[j][start + i:start + i + 1, :]
            work = work - factor * work[k:k + 1, :]
    pivots = jnp.sum(jnp.where(row_id == lane_id, work, 0.0), axis=1, keepdims=True)
    inverse = work[:, COLS:] / jnp.sqrt(pivots)
    load.wait()
    for b in range(OWN):
        out_ref[b] = lax.dot_general(
            inverse, image_ref[:, b * ROWS:(b + 1) * ROWS], NN,
            precision=lax.Precision.HIGHEST, preferred_element_type=jnp.float32,
        )


def solve(documents, gram, other, image):
    vmem = pl.BlockSpec(memory_space=pltpu.VMEM)
    return pl.pallas_call(
        functools.partial(solve_kernel, float(documents)),
        out_shape=jax.ShapeDtypeStruct((OWN, COLS, ROWS), jnp.float32),
        in_specs=[vmem, vmem, pl.BlockSpec(memory_space=pltpu.HBM)],
        scratch_shapes=[pltpu.VMEM((COLS, DOCS), jnp.float32), pltpu.SemaphoreType.DMA],
        compiler_params=pltpu.CompilerParams(vmem_limit_bytes=SMALL_LIMIT),
        name="solve",
    )(gram, other, image)


def shift_z(k):
    return [(y * SIDE + z, y * SIDE + (z + k) % SIDE) for y in range(SIDE) for z in range(SIDE)]


def shift_y(k):
    return [(y * SIDE + z, (y + k) % SIDE * SIDE + z) for y in range(SIDE) for z in range(SIDE)]


def per_device(embedding, subspace, degree, neighbours, counts):
    position = lax.axis_index("blk")
    y, z = position // SIDE, position % SIDE
    row_ids = jnp.stack([(y * SIDE + (z + k) % SIDE) * OWN + UNIT * h + i for k, h in ARRIVAL for i in range(UNIT)])
    col_ids = jnp.stack([((y + k) % SIDE * SIDE + z) * OWN + UNIT * h + i for k, h in ARRIVAL for i in range(UNIT)])
    index = jnp.stack([row_ids, col_ids]).astype(jnp.int32)

    z_a, z_b, y_a, y_b = prepare(embedding, subspace, degree, neighbours, counts)

    def gather(a, b, shift):
        minus_a = lax.ppermute(a, "blk", shift(1))
        plus_b = lax.ppermute(b, "blk", shift(-1))
        b_next, minus_a = lax.optimization_barrier((b, minus_a))
        a_next, plus_b = lax.optimization_barrier((a, plus_b))
        minus_b = lax.ppermute(b_next, "blk", shift(1))
        plus_a = lax.ppermute(a_next, "blk", shift(-1))
        minus_next, minus_b = lax.optimization_barrier((minus_a, minus_b))
        plus_next, plus_a = lax.optimization_barrier((plus_b, plus_a))
        far_a = lax.ppermute(minus_next, "blk", shift(1))
        far_b = lax.ppermute(plus_next, "blk", shift(-1))
        return a, b, minus_a, plus_b, minus_b, plus_a, far_a, far_b

    z_parts = gather(z_a, z_b, shift_z)
    y_parts = gather(y_a, y_b, shift_y)
    acc = stage(0, 4, index, z_parts, y_parts)
    acc = stage(4, 6, index, z_parts, y_parts, acc)
    own, to_minus, to_plus, to_far = stage(6, 8, index, z_parts, y_parts, acc)
    back_a = lax.ppermute(to_minus, "blk", shift_z(-1))
    back_b = lax.ppermute(to_plus, "blk", shift_z(1))
    back_c = lax.ppermute(to_far, "blk", shift_z(2))
    image, gram = finish(degree, own, back_a, back_b, back_c)

    devices_blk = lax.axis_size("blk")
    devices_dp = lax.axis_size("dp")
    other = lax.ppermute(gram, "dp", [(i, i ^ 1) for i in range(devices_dp)])
    for axis, size, first in (("dp", devices_dp, 2), ("blk", devices_blk, 1)):
        step = first
        while step < size:
            gram = gram + other
            other = lax.ppermute(gram, axis, [(i, i ^ step) for i in range(size)])
            step *= 2
    solved = solve(DOCS * devices_blk * devices_dp, gram, other, image)
    return jnp.swapaxes(solved, 1, 2)


def solution(mesh):
    placed = (
        P(("dp", "blk"), None, None),
        P(("dp", "blk"), None, None),
        P(("dp", "blk"), None),
        P(("dp", "blk"), None),
        P(("dp", "blk")),
    )
    return jax.shard_map(
        per_device,
        mesh=mesh,
        in_specs=placed,
        out_specs=P(("dp", "blk"), None, None),
        check_vma=False,
    )
```

```python
import functools
import math

import jax
import jax.numpy as jnp
from jax import lax
from jax.experimental import pallas as pl
from jax.experimental.pallas import tpu as pltpu
from jax.sharding import PartitionSpec as P

ROWS = 256
FEAT = 1024
COLS = 64
OWN = 4
SIDE = 4
HALF = OWN // 2 * ROWS
DOCS = OWN * ROWS
META = 16
SCALED = 32
UNIT = 2
UNITS = 2 * SIDE
Z_ROWS = META + HALF
Y_X = SCALED + META
Y_ROWS = Y_X + HALF
GROUPED = 8
VMEM_LIMIT = 62 * 2**20
SMALL_LIMIT = 16 * 2**20
PANEL = 8
ARRIVAL = ((0, 0), (0, 1), (-1, 0), (1, 1), (-1, 1), (1, 0), (2, 0), (2, 1))
LOG2E = 1.4426950408889634
GAIN = 2.0 * LOG2E / (4.0 * math.sqrt(FEAT))
BIAS = 2.0 * FEAT * LOG2E / (4.0 * math.sqrt(FEAT))
SQ_GAIN = -LOG2E / (4.0 * math.sqrt(FEAT))

NT = (((1,), (1,)), ((), ()))
NN = (((1,), (0,)), ((), ()))


def dot(a, b, dims):
    return lax.dot_general(a, b, dims, preferred_element_type=jnp.float32)


def prep_kernel(nbr_hbm, cnt_hbm, x_hbm, sub_hbm, deg_hbm, za_ref, zb_ref, ya_ref, yb_ref,
                nbr_ref, cnt_ref, x_ref, sub_ref, deg_ref, small, sems):
    loads = [
        pltpu.make_async_copy(x_hbm.at[pl.ds(b * ROWS, ROWS)], x_ref.at[pl.ds(b * ROWS, ROWS)], sems.at[b])
        for b in range(OWN)
    ]
    extra = [
        pltpu.make_async_copy(nbr_hbm, nbr_ref, sems.at[4]),
        pltpu.make_async_copy(cnt_hbm, cnt_ref, sems.at[5]),
        pltpu.make_async_copy(deg_hbm, deg_ref, sems.at[6]),
        pltpu.make_async_copy(sub_hbm, sub_ref, sems.at[7]),
    ]
    for copy in loads + extra:
        copy.start()
    stores = []

    def store(source, target, which):
        copy = pltpu.make_async_copy(source, target, sems.at[which])
        copy.start()
        stores.append(copy)

    ones = jnp.ones((META, FEAT), jnp.bfloat16)
    squares = []
    for b in range(OWN):
        half, place = b // UNIT, b % UNIT * ROWS
        loads[b].wait()
        source = x_ref.at[pl.ds(b * ROWS, ROWS)]
        store(source, (za_ref, zb_ref)[half].at[pl.ds(META + place, ROWS)], 8 + b)
        store(source, (ya_ref, yb_ref)[half].at[pl.ds(Y_X + place, ROWS)], 12 + b)
        x = x_ref[b * ROWS:(b + 1) * ROWS, :].astype(jnp.float32)
        sq = x * x
        high = sq.astype(jnp.bfloat16)
        low = (sq - high.astype(jnp.float32)).astype(jnp.bfloat16)
        squares.append(dot(ones, high, NT) + dot(ones, low, NT))
    for copy in extra:
        copy.wait()
    lane = lax.broadcasted_iota(jnp.int32, (1, 128), 1)
    which = lax.broadcasted_iota(jnp.int32, (META, FEAT), 0)
    pad = jnp.zeros((1, FEAT - 128), jnp.float32)
    for half in range(2):
        total = jnp.concatenate(squares[half * UNIT:(half + 1) * UNIT] + [jnp.zeros((META, FEAT - HALF), jnp.float32)], axis=1)
        s_high = total.astype(jnp.bfloat16).astype(jnp.float32)
        rest = total - s_high
        s_mid = rest.astype(jnp.bfloat16).astype(jnp.float32)
        s_low = rest - s_mid
        meta = jnp.where(which == 0, s_high, jnp.where(which == 1, s_mid, jnp.where(which == 2, s_low, 0.0)))
        for i in range(UNIT):
            b = half * UNIT + i
            row = jnp.zeros((1, 128), jnp.float32)
            for k in range(nbr_ref.shape[1]):
                used = (k < cnt_ref[b]).astype(jnp.float32)
                row = row + jnp.where(lane == nbr_ref[b, k], used, 0.0)
            meta = jnp.where(which == 4 + i, jnp.concatenate([row, pad], axis=1), meta)
            inv = 1.0 / jnp.sqrt(deg_ref[b:b + 1, :])
            scaled = (sub_ref[b] * inv).astype(jnp.bfloat16)
            small[half, 16 * i:16 * (i + 1), :] = jnp.concatenate(
                [scaled[16 * g:16 * (g + 1), :] for g in range(4)], axis=1
            )
        small[half, SCALED:Y_X, :] = meta.astype(jnp.bfloat16)
        store(small.at[half], (ya_ref, yb_ref)[half].at[pl.ds(0, Y_X)], 16 + half)
        store(small.at[half, pl.ds(SCALED, META)], (za_ref, zb_ref)[half].at[pl.ds(0, META)], 18 + half)
    for copy in stores:
        copy.wait()


def prepare(embedding, subspace, degree, neighbours, counts):
    hbm = pl.BlockSpec(memory_space=pltpu.HBM)
    return pl.pallas_call(
        prep_kernel,
        out_shape=(jax.ShapeDtypeStruct((Z_ROWS, FEAT), jnp.bfloat16),) * 2
        + (jax.ShapeDtypeStruct((Y_ROWS, FEAT), jnp.bfloat16),) * 2,
        in_specs=[hbm] * 5,
        out_specs=(hbm,) * 4,
        scratch_shapes=[
            pltpu.SMEM(neighbours.shape, jnp.int32),
            pltpu.SMEM(counts.shape, jnp.int32),
            pltpu.VMEM((DOCS, FEAT), jnp.bfloat16),
            pltpu.VMEM((OWN, COLS, ROWS), jnp.float32),
            pltpu.VMEM((OWN, ROWS), jnp.float32),
            pltpu.VMEM((2, Y_X, FEAT), jnp.bfloat16),
            pltpu.SemaphoreType.DMA((20,)),
        ],
        compiler_params=pltpu.CompilerParams(vmem_limit_bytes=VMEM_LIMIT),
        name="prepare",
    )(neighbours, counts, embedding.reshape(DOCS, FEAT), jnp.swapaxes(subspace, 1, 2), degree)


def stage_kernel(old, new, last, *refs):
    z_refs = refs[:new]
    y_refs = refs[new:2 * new]
    rest = refs[2 * new:]
    if old:
        acc_in, rest = rest[0], rest[1:]
    if last:
        outs, rest = rest[:4], rest[4:]
    else:
        acc_out, rest = rest[0], rest[1:]
    (r_x, c_x, c_s, c_pack, meta_r, meta_c, sq_r, sq_c, col, adj_vmem, adj_r, adj_c, idx_ref, codes, edge_list, acc,
     sem_r, sem_c, sem_s, sem_m, sem_n, sem_a) = rest
    old_slots, slots = UNIT * old, UNIT * new

    meta_copies = []
    pack_copies = []
    r_copies = []
    c_copies = []
    for u in range(new):
        meta_copies.append(pltpu.make_async_copy(z_refs[u].at[pl.ds(0, META)], meta_r.at[u], sem_m.at[u]))
        meta_copies.append(pltpu.make_async_copy(y_refs[u].at[pl.ds(SCALED, META)], meta_c.at[u], sem_n.at[u]))
        pack_copies.append(pltpu.make_async_copy(y_refs[u].at[pl.ds(0, SCALED)], c_pack.at[u], sem_s.at[u]))
        r_copies.append(pltpu.make_async_copy(z_refs[u].at[pl.ds(META, HALF)], r_x.at[u], sem_r.at[u]))
        c_copies.append(pltpu.make_async_copy(y_refs[u].at[pl.ds(Y_X, HALF)], c_x.at[u], sem_c.at[u]))
    if old:
        acc_copy = pltpu.make_async_copy(acc_in, acc, sem_a.at[2])
    if old:
        sweeps = [
            ((0, old_slots, old_slots, slots), r_copies[old:] + c_copies[:old]),
            ((old_slots, slots, 0, slots), c_copies[old:] + r_copies[:old]),
        ]
    else:
        sweeps = [((0, slots, 0, slots), c_copies + r_copies)]
    for copy in meta_copies:
        copy.start()
    for copy in sweeps[0][1] + pack_copies:
        copy.start()
    if old:
        acc_copy.start()

    position = lax.axis_index("blk")
    y, z = lax.div(position, SIDE), lax.rem(position, SIDE)
    for u in range(new):
        offset, half = ARRIVAL[u]
        for i in range(UNIT):
            place = UNIT * half + i
            idx_ref[0, u * UNIT + i] = (y * SIDE + lax.rem(z + offset + SIDE, SIDE)) * OWN + place
            idx_ref[1, u * UNIT + i] = (lax.rem(y + offset + SIDE, SIDE) * SIDE + z) * OWN + place

    for copy in meta_copies:
        copy.wait()
    for side, (meta, keep, adj) in enumerate(((meta_r, sq_r, adj_r), (meta_c, sq_c, adj_c))):
        for u in range(new):
            m = meta[u].astype(jnp.float32)
            total = (m[0:1, 0:HALF] + m[1:2, 0:HALF] + m[2:3, 0:HALF]) * SQ_GAIN
            for i in range(UNIT):
                piece = total[:, i * ROWS:(i + 1) * ROWS]
                if side == 0:
                    keep[u * UNIT + i] = piece + BIAS
                else:
                    keep[u * UNIT + i:u * UNIT + i + 1, :] = piece
            adj_vmem[side, u * UNIT:(u + 1) * UNIT, :] = m[4:4 + UNIT, 0:128].astype(jnp.int32)
        pltpu.make_async_copy(adj_vmem.at[side], adj, sem_a.at[side]).start()
    columns = jnp.transpose(sq_c[...])
    for s in range(slots):
        col[s] = jnp.broadcast_to(columns[:, s:s + 1], (ROWS, 128))
    for copy in pack_copies:
        copy.wait()
    for s in range(slots):
        p = c_pack[s // UNIT, 16 * (s % UNIT):16 * (s % UNIT + 1), :]
        c_s[s] = jnp.concatenate([p[:, ROWS * k:ROWS * (k + 1)] for k in range(4)], axis=0)
    for side, adj in enumerate((adj_r, adj_c)):
        pltpu.make_async_copy(adj_vmem.at[side], adj, sem_a.at[side]).wait()

    def form(pairs, diagonal):
        cross = [
            dot(c_x[c // UNIT, pl.ds(c % UNIT * ROWS, ROWS), :], r_x[r // UNIT, pl.ds(r % UNIT * ROWS, ROWS), :], NT)
            for c, r, _ in pairs
        ]
        terms = []
        for (c, r, weight), value in zip(pairs, cross):
            bias = jnp.concatenate([col[c], col[c]], axis=1) + sq_r[r]
            tile = jnp.exp2(value * GAIN + bias)
            if diagonal:
                row_id = lax.broadcasted_iota(jnp.int32, (ROWS, ROWS), 0)
                col_id = lax.broadcasted_iota(jnp.int32, (ROWS, ROWS), 1)
                tile = jnp.where(row_id == col_id, 0.0, tile)
            term = dot(c_s[c], tile.astype(jnp.bfloat16), NN)
            terms.append(term if diagonal else term * weight)
        for (c, r, _), term in zip(pairs, terms):
            acc[r] = acc[r] + term

    def list_tiles(c_lo, c_hi, r_lo, r_hi):
        def per_c(c, count):
            block_c = idx_ref[1, c]
            for r in range(r_lo, r_hi):
                edges = adj_r[r, block_c] + adj_c[c, idx_ref[0, r]]
                codes[count] = c * 16 + r
                edge_list[count] = edges
                count = count + (edges > 0).astype(jnp.int32)
            return count

        count = lax.fori_loop(c_lo, c_hi, per_c, 0)
        for i in range(GROUPED - 1):
            codes[count + i] = codes[0]
            edge_list[count + i] = 0
        return count

    def run_tiles(count):
        def step(t, carry):
            pairs = []
            for i in range(GROUPED):
                code = codes[t * GROUPED + i]
                pairs.append((code // 16, code % 16, edge_list[t * GROUPED + i].astype(jnp.float32)))
            form(pairs, False)
            return carry

        lax.fori_loop(0, (count + GROUPED - 1) // GROUPED, step, 0)

    if old:
        acc_copy.wait()
    else:
        acc[...] = jnp.zeros_like(acc)
    for which, (span, loads) in enumerate(sweeps):
        count = list_tiles(*span)
        for copy in loads:
            copy.wait()
        if which + 1 < len(sweeps):
            for copy in sweeps[which + 1][1]:
                copy.start()
        if not old:
            form([(s, s, None) for s in range(OWN)], True)
        run_tiles(count)
    if last:
        for out, order in zip(outs, ((0, 1, 2, 3), (4, 5, 8, 9), (10, 11, 6, 7), (12, 13, 14, 15))):
            for k, s in enumerate(order):
                out[k] = acc[s].astype(out.dtype)
    else:
        acc_out[...] = acc[...]


def stage(old, new, z_parts, y_parts, acc=None):
    vmem = pl.BlockSpec(memory_space=pltpu.VMEM)
    hbm = pl.BlockSpec(memory_space=pltpu.HBM)
    last = new == UNITS
    operands = [*z_parts[:new], *y_parts[:new]]
    in_specs = [hbm] * (2 * new)
    if old:
        operands.append(acc)
        in_specs.append(hbm)
    if last:
        out_shape = tuple(
            jax.ShapeDtypeStruct((OWN, COLS, ROWS), kind) for kind in (jnp.float32,) * 4
        )
        out_specs = (vmem,) * 4
    else:
        out_shape = jax.ShapeDtypeStruct((16, COLS, ROWS), jnp.float32)
        out_specs = vmem
    slots = UNIT * new
    return pl.pallas_call(
        functools.partial(stage_kernel, old, new, last),
        out_shape=out_shape,
        in_specs=in_specs,
        out_specs=out_specs,
        scratch_shapes=[
            pltpu.VMEM((new, HALF, FEAT), jnp.bfloat16),
            pltpu.VMEM((new, HALF, FEAT), jnp.bfloat16),
            pltpu.VMEM((slots, COLS, ROWS), jnp.bfloat16),
            pltpu.VMEM((new, SCALED, FEAT), jnp.bfloat16),
            pltpu.VMEM((new, META, FEAT), jnp.bfloat16),
            pltpu.VMEM((new, META, FEAT), jnp.bfloat16),
            pltpu.VMEM((slots, 1, ROWS), jnp.float32),
            pltpu.VMEM((128, ROWS), jnp.float32),
            pltpu.VMEM((slots, ROWS, 128), jnp.float32),
            pltpu.VMEM((2, 16, 128), jnp.int32),
            pltpu.SMEM((16, 128), jnp.int32),
            pltpu.SMEM((16, 128), jnp.int32),
            pltpu.SMEM((2, 16), jnp.int32),
            pltpu.SMEM((264,), jnp.int32),
            pltpu.SMEM((264,), jnp.int32),
            pltpu.VMEM((16, COLS, ROWS), jnp.float32),
            pltpu.SemaphoreType.DMA((new,)),
            pltpu.SemaphoreType.DMA((new,)),
            pltpu.SemaphoreType.DMA((new,)),
            pltpu.SemaphoreType.DMA((new,)),
            pltpu.SemaphoreType.DMA((new,)),
            pltpu.SemaphoreType.DMA((3,)),
        ],
        compiler_params=pltpu.CompilerParams(vmem_limit_bytes=VMEM_LIMIT),
        cost_estimate=pl.CostEstimate(flops=6 * 10**9, bytes_accessed=16 * 2**20, transcendentals=10**6),
        name="stage_%d" % new,
    )(*operands)


def finish_kernel(deg_ref, own_ref, a_ref, b_ref, c_ref, image_ref, gram_ref):
    parts = []
    for b in range(OWN):
        inv = 1.0 / jnp.sqrt(deg_ref[b:b + 1, :])
        far = [ref[b].astype(jnp.float32) for ref in (a_ref, b_ref, c_ref)]
        parts.append((own_ref[b] + far[0] + (far[1] + far[2])) * inv)
    image = jnp.concatenate(parts, axis=1)
    image_ref[...] = image
    gram = lax.dot_general(
        image, image, NT, precision=lax.Precision.HIGHEST, preferred_element_type=jnp.float32
    )
    gram_ref[...] = jnp.concatenate([gram[:COLS // 2], gram[COLS // 2:]], axis=1)


def finish(degree, own, a, b, c):
    return pl.pallas_call(
        finish_kernel,
        out_shape=(
            jax.ShapeDtypeStruct((COLS, DOCS), jnp.float32),
            jax.ShapeDtypeStruct((COLS // 2, 2 * COLS), jnp.float32),
        ),
        compiler_params=pltpu.CompilerParams(vmem_limit_bytes=SMALL_LIMIT),
        name="finish",
    )(degree, own, a, b, c)


def solve_kernel(documents, gram_ref, other_ref, image_hbm, out_ref, image_ref, sem):
    load = pltpu.make_async_copy(image_hbm, image_ref, sem)
    load.start()
    packed = (gram_ref[...] + other_ref[...]) / documents
    gram = jnp.concatenate([packed[:, :COLS], packed[:, COLS:]], axis=0)
    row_id = lax.broadcasted_iota(jnp.int32, (COLS, 2 * COLS), 0)
    lane_id = lax.broadcasted_iota(jnp.int32, (COLS, 2 * COLS), 1)
    unit = (row_id[:, :COLS] == lane_id[:, :COLS]).astype(jnp.float32)
    work = jnp.concatenate([gram, unit], axis=1)
    for start in range(0, COLS, PANEL):
        columns = [jnp.broadcast_to(work[:, start + j:start + j + 1], work.shape) for j in range(PANEL)]
        for j in range(PANEL):
            k = start + j
            factor = columns[j] * (1.0 / columns[j][k:k + 1, :])
            factor = jnp.where(row_id > k, factor, 0.0)
            for i in range(j + 1, PANEL):
                columns[i] = columns[i] - factor * columns[j][start + i:start + i + 1, :]
            work = work - factor * work[k:k + 1, :]
    pivots = jnp.sum(jnp.where(row_id == lane_id, work, 0.0), axis=1, keepdims=True)
    inverse = work[:, COLS:] / jnp.sqrt(pivots)
    load.wait()
    for b in range(OWN):
        out_ref[b] = lax.dot_general(
            inverse, image_ref[:, b * ROWS:(b + 1) * ROWS], NN,
            precision=lax.Precision.HIGHEST, preferred_element_type=jnp.float32,
        )


def solve(documents, gram, other, image):
    vmem = pl.BlockSpec(memory_space=pltpu.VMEM)
    return pl.pallas_call(
        functools.partial(solve_kernel, float(documents)),
        out_shape=jax.ShapeDtypeStruct((OWN, COLS, ROWS), jnp.float32),
        in_specs=[vmem, vmem, pl.BlockSpec(memory_space=pltpu.HBM)],
        scratch_shapes=[pltpu.VMEM((COLS, DOCS), jnp.float32), pltpu.SemaphoreType.DMA],
        compiler_params=pltpu.CompilerParams(vmem_limit_bytes=SMALL_LIMIT),
        name="solve",
    )(gram, other, image)


def shift_z(k):
    return [(y * SIDE + z, y * SIDE + (z + k) % SIDE) for y in range(SIDE) for z in range(SIDE)]


def shift_y(k):
    return [(y * SIDE + z, (y + k) % SIDE * SIDE + z) for y in range(SIDE) for z in range(SIDE)]


def per_device(embedding, subspace, degree, neighbours, counts):
    z_a, z_b, y_a, y_b = prepare(embedding, subspace, degree, neighbours, counts)

    def gather(a, b, shift):
        minus_a = lax.ppermute(a, "blk", shift(1))
        plus_b = lax.ppermute(b, "blk", shift(-1))
        b_next, minus_a = lax.optimization_barrier((b, minus_a))
        a_next, plus_b = lax.optimization_barrier((a, plus_b))
        minus_b = lax.ppermute(b_next, "blk", shift(1))
        plus_a = lax.ppermute(a_next, "blk", shift(-1))
        minus_next, minus_b = lax.optimization_barrier((minus_a, minus_b))
        plus_next, plus_a = lax.optimization_barrier((plus_b, plus_a))
        far_a = lax.ppermute(minus_next, "blk", shift(1))
        far_b = lax.ppermute(plus_next, "blk", shift(-1))
        return a, b, minus_a, plus_b, minus_b, plus_a, far_a, far_b

    z_parts = gather(z_a, z_b, shift_z)
    y_parts = gather(y_a, y_b, shift_y)
    acc = stage(0, 4, z_parts, y_parts)
    acc = stage(4, 6, z_parts, y_parts, acc)
    own, to_minus, to_plus, to_far = stage(6, 8, z_parts, y_parts, acc)
    back_a = lax.ppermute(to_minus, "blk", shift_z(-1))
    back_b = lax.ppermute(to_plus, "blk", shift_z(1))
    back_c = lax.ppermute(to_far, "blk", shift_z(2))
    image, gram = finish(degree, own, back_a, back_b, back_c)

    devices_blk = lax.axis_size("blk")
    devices_dp = lax.axis_size("dp")
    other = lax.ppermute(gram, "dp", [(i, i ^ 1) for i in range(devices_dp)])
    for axis, size, first in (("dp", devices_dp, 2), ("blk", devices_blk, 1)):
        step = first
        while step < size:
            gram = gram + other
            other = lax.ppermute(gram, axis, [(i, i ^ step) for i in range(size)])
            step *= 2
    solved = solve(DOCS * devices_blk * devices_dp, gram, other, image)
    return jnp.swapaxes(solved, 1, 2)


def solution(mesh):
    placed = (
        P(("dp", "blk"), None, None),
        P(("dp", "blk"), None, None),
        P(("dp", "blk"), None),
        P(("dp", "blk"), None),
        P(("dp", "blk")),
    )
    return jax.shard_map(
        per_device,
        mesh=mesh,
        in_specs=placed,
        out_specs=P(("dp", "blk"), None, None),
        check_vma=False,
    )
```

```python
import functools
import math

import jax
import jax.numpy as jnp
from jax import lax
from jax.experimental import pallas as pl
from jax.experimental.pallas import tpu as pltpu
from jax.sharding import PartitionSpec as P

ROWS = 256
FEAT = 1024
COLS = 64
OWN = 4
SIDE = 4
HALF = OWN // 2 * ROWS
DOCS = OWN * ROWS
META = 16
SCALED = 32
UNIT = 2
UNITS = 2 * SIDE
Z_ROWS = META + HALF
Y_X = SCALED + META
Y_ROWS = Y_X + HALF
GROUPED = 8
VMEM_LIMIT = 62 * 2**20
SMALL_LIMIT = 16 * 2**20
PANEL = 16
ARRIVAL = ((0, 0), (0, 1), (-1, 0), (1, 1), (-1, 1), (1, 0), (2, 0), (2, 1))
LOG2E = 1.4426950408889634
GAIN = 2.0 * LOG2E / (4.0 * math.sqrt(FEAT))
BIAS = 2.0 * FEAT * LOG2E / (4.0 * math.sqrt(FEAT))
SQ_GAIN = -LOG2E / (4.0 * math.sqrt(FEAT))

NT = (((1,), (1,)), ((), ()))
NN = (((1,), (0,)), ((), ()))


def dot(a, b, dims):
    return lax.dot_general(a, b, dims, preferred_element_type=jnp.float32)


def prep_kernel(nbr_hbm, cnt_hbm, x_hbm, sub_hbm, deg_hbm, za_ref, zb_ref, ya_ref, yb_ref,
                nbr_ref, cnt_ref, x_ref, sub_ref, deg_ref, small, sems):
    loads = [
        pltpu.make_async_copy(x_hbm.at[pl.ds(b * ROWS, ROWS)], x_ref.at[pl.ds(b * ROWS, ROWS)], sems.at[b])
        for b in range(OWN)
    ]
    extra = [
        pltpu.make_async_copy(nbr_hbm, nbr_ref, sems.at[4]),
        pltpu.make_async_copy(cnt_hbm, cnt_ref, sems.at[5]),
        pltpu.make_async_copy(deg_hbm, deg_ref, sems.at[6]),
        pltpu.make_async_copy(sub_hbm, sub_ref, sems.at[7]),
    ]
    for copy in loads + extra:
        copy.start()
    stores = []

    def store(source, target, which):
        copy = pltpu.make_async_copy(source, target, sems.at[which])
        copy.start()
        stores.append(copy)

    ones = jnp.ones((META, FEAT), jnp.bfloat16)
    squares = []
    for b in range(OWN):
        half, place = b // UNIT, b % UNIT * ROWS
        loads[b].wait()
        source = x_ref.at[pl.ds(b * ROWS, ROWS)]
        store(source, (za_ref, zb_ref)[half].at[pl.ds(META + place, ROWS)], 8 + b)
        store(source, (ya_ref, yb_ref)[half].at[pl.ds(Y_X + place, ROWS)], 12 + b)
        x = x_ref[b * ROWS:(b + 1) * ROWS, :].astype(jnp.float32)
        sq = x * x
        high = sq.astype(jnp.bfloat16)
        low = (sq - high.astype(jnp.float32)).astype(jnp.bfloat16)
        squares.append(dot(ones, high, NT) + dot(ones, low, NT))
    for copy in extra:
        copy.wait()
    lane = lax.broadcasted_iota(jnp.int32, (1, 128), 1)
    which = lax.broadcasted_iota(jnp.int32, (META, FEAT), 0)
    pad = jnp.zeros((1, FEAT - 128), jnp.float32)
    for half in range(2):
        total = jnp.concatenate(squares[half * UNIT:(half + 1) * UNIT] + [jnp.zeros((META, FEAT - HALF), jnp.float32)], axis=1)
        s_high = total.astype(jnp.bfloat16).astype(jnp.float32)
        rest = total - s_high
        s_mid = rest.astype(jnp.bfloat16).astype(jnp.float32)
        s_low = rest - s_mid
        meta = jnp.where(which == 0, s_high, jnp.where(which == 1, s_mid, jnp.where(which == 2, s_low, 0.0)))
        for i in range(UNIT):
            b = half * UNIT + i
            row = jnp.zeros((1, 128), jnp.float32)
            for k in range(nbr_ref.shape[1]):
                used = (k < cnt_ref[b]).astype(jnp.float32)
                row = row + jnp.where(lane == nbr_ref[b, k], used, 0.0)
            meta = jnp.where(which == 4 + i, jnp.concatenate([row, pad], axis=1), meta)
            inv = 1.0 / jnp.sqrt(deg_ref[b:b + 1, :])
            scaled = (sub_ref[b] * inv).astype(jnp.bfloat16)
            small[half, 16 * i:16 * (i + 1), :] = jnp.concatenate(
                [scaled[16 * g:16 * (g + 1), :] for g in range(4)], axis=1
            )
        small[half, SCALED:Y_X, :] = meta.astype(jnp.bfloat16)
        store(small.at[half], (ya_ref, yb_ref)[half].at[pl.ds(0, Y_X)], 16 + half)
        store(small.at[half, pl.ds(SCALED, META)], (za_ref, zb_ref)[half].at[pl.ds(0, META)], 18 + half)
    for copy in stores:
        copy.wait()


def prepare(embedding, subspace, degree, neighbours, counts):
    hbm = pl.BlockSpec(memory_space=pltpu.HBM)
    return pl.pallas_call(
        prep_kernel,
        out_shape=(jax.ShapeDtypeStruct((Z_ROWS, FEAT), jnp.bfloat16),) * 2
        + (jax.ShapeDtypeStruct((Y_ROWS, FEAT), jnp.bfloat16),) * 2,
        in_specs=[hbm] * 5,
        out_specs=(hbm,) * 4,
        scratch_shapes=[
            pltpu.SMEM(neighbours.shape, jnp.int32),
            pltpu.SMEM(counts.shape, jnp.int32),
            pltpu.VMEM((DOCS, FEAT), jnp.bfloat16),
            pltpu.VMEM((OWN, COLS, ROWS), jnp.float32),
            pltpu.VMEM((OWN, ROWS), jnp.float32),
            pltpu.VMEM((2, Y_X, FEAT), jnp.bfloat16),
            pltpu.SemaphoreType.DMA((20,)),
        ],
        compiler_params=pltpu.CompilerParams(vmem_limit_bytes=VMEM_LIMIT),
        name="prepare",
    )(neighbours, counts, embedding.reshape(DOCS, FEAT), jnp.swapaxes(subspace, 1, 2), degree)


def stage_kernel(old, new, last, *refs):
    z_refs = refs[:new]
    y_refs = refs[new:2 * new]
    rest = refs[2 * new:]
    if old:
        acc_in, rest = rest[0], rest[1:]
    if last:
        outs, rest = rest[:4], rest[4:]
    else:
        acc_out, rest = rest[0], rest[1:]
    (r_x, c_x, c_s, c_pack, meta_r, meta_c, sq_r, sq_c, col, adj_vmem, adj_r, adj_c, idx_ref, codes, edge_list, acc,
     sem_r, sem_c, sem_s, sem_m, sem_n, sem_a) = rest
    old_slots, slots = UNIT * old, UNIT * new

    meta_copies = []
    pack_copies = []
    r_copies = []
    c_copies = []
    for u in range(new):
        meta_copies.append(pltpu.make_async_copy(z_refs[u].at[pl.ds(0, META)], meta_r.at[u], sem_m.at[u]))
        meta_copies.append(pltpu.make_async_copy(y_refs[u].at[pl.ds(SCALED, META)], meta_c.at[u], sem_n.at[u]))
        pack_copies.append(pltpu.make_async_copy(y_refs[u].at[pl.ds(0, SCALED)], c_pack.at[u], sem_s.at[u]))
        r_copies.append(pltpu.make_async_copy(z_refs[u].at[pl.ds(META, HALF)], r_x.at[u], sem_r.at[u]))
        c_copies.append(pltpu.make_async_copy(y_refs[u].at[pl.ds(Y_X, HALF)], c_x.at[u], sem_c.at[u]))
    if old:
        acc_copy = pltpu.make_async_copy(acc_in, acc, sem_a.at[2])
    if old:
        sweeps = [
            ((0, old_slots, old_slots, slots), r_copies[old:] + c_copies[:old]),
            ((old_slots, slots, 0, slots), c_copies[old:] + r_copies[:old]),
        ]
    else:
        sweeps = [((0, slots, 0, slots), c_copies + r_copies)]
    for copy in meta_copies:
        copy.start()
    for copy in sweeps[0][1] + pack_copies:
        copy.start()
    if old:
        acc_copy.start()

    position = lax.axis_index("blk")
    y, z = lax.div(position, SIDE), lax.rem(position, SIDE)
    for u in range(new):
        offset, half = ARRIVAL[u]
        for i in range(UNIT):
            place = UNIT * half + i
            idx_ref[0, u * UNIT + i] = (y * SIDE + lax.rem(z + offset + SIDE, SIDE)) * OWN + place
            idx_ref[1, u * UNIT + i] = (lax.rem(y + offset + SIDE, SIDE) * SIDE + z) * OWN + place

    for copy in meta_copies:
        copy.wait()
    for side, (meta, keep, adj) in enumerate(((meta_r, sq_r, adj_r), (meta_c, sq_c, adj_c))):
        for u in range(new):
            m = meta[u].astype(jnp.float32)
            total = (m[0:1, 0:HALF] + m[1:2, 0:HALF] + m[2:3, 0:HALF]) * SQ_GAIN
            for i in range(UNIT):
                piece = total[:, i * ROWS:(i + 1) * ROWS]
                if side == 0:
                    keep[u * UNIT + i] = piece + BIAS
                else:
                    keep[u * UNIT + i:u * UNIT + i + 1, :] = piece
            adj_vmem[side, u * UNIT:(u + 1) * UNIT, :] = m[4:4 + UNIT, 0:128].astype(jnp.int32)
        pltpu.make_async_copy(adj_vmem.at[side], adj, sem_a.at[side]).start()
    columns = jnp.transpose(sq_c[...])
    for s in range(slots):
        col[s] = jnp.broadcast_to(columns[:, s:s + 1], (ROWS, 128))
    for copy in pack_copies:
        copy.wait()
    for s in range(slots):
        p = c_pack[s // UNIT, 16 * (s % UNIT):16 * (s % UNIT + 1), :]
        c_s[s] = jnp.concatenate([p[:, ROWS * k:ROWS * (k + 1)] for k in range(4)], axis=0)
    for side, adj in enumerate((adj_r, adj_c)):
        pltpu.make_async_copy(adj_vmem.at[side], adj, sem_a.at[side]).wait()

    def form(pairs, diagonal):
        cross = [
            dot(c_x[c // UNIT, pl.ds(c % UNIT * ROWS, ROWS), :], r_x[r // UNIT, pl.ds(r % UNIT * ROWS, ROWS), :], NT)
            for c, r, _ in pairs
        ]
        terms = []
        for (c, r, weight), value in zip(pairs, cross):
            bias = jnp.concatenate([col[c], col[c]], axis=1) + sq_r[r]
            tile = jnp.exp2(value * GAIN + bias)
            if diagonal:
                row_id = lax.broadcasted_iota(jnp.int32, (ROWS, ROWS), 0)
                col_id = lax.broadcasted_iota(jnp.int32, (ROWS, ROWS), 1)
                tile = jnp.where(row_id == col_id, 0.0, tile)
            term = dot(c_s[c], tile.astype(jnp.bfloat16), NN)
            terms.append(term if diagonal else term * weight)
        for (c, r, _), term in zip(pairs, terms):
            acc[r] = acc[r] + term

    def list_tiles(c_lo, c_hi, r_lo, r_hi):
        def per_c(c, count):
            block_c = idx_ref[1, c]
            for r in range(r_lo, r_hi):
                edges = adj_r[r, block_c] + adj_c[c, idx_ref[0, r]]
                codes[count] = c * 16 + r
                edge_list[count] = edges
                count = count + (edges > 0).astype(jnp.int32)
            return count

        count = lax.fori_loop(c_lo, c_hi, per_c, 0)
        for i in range(GROUPED - 1):
            codes[count + i] = codes[0]
            edge_list[count + i] = 0
        return count

    def run_tiles(count):
        def step(t, carry):
            pairs = []
            for i in range(GROUPED):
                code = codes[t * GROUPED + i]
                pairs.append((code // 16, code % 16, edge_list[t * GROUPED + i].astype(jnp.float32)))
            form(pairs, False)
            return carry

        lax.fori_loop(0, (count + GROUPED - 1) // GROUPED, step, 0)

    if old:
        acc_copy.wait()
    else:
        acc[...] = jnp.zeros_like(acc)
    for which, (span, loads) in enumerate(sweeps):
        count = list_tiles(*span)
        for copy in loads:
            copy.wait()
        if which + 1 < len(sweeps):
            for copy in sweeps[which + 1][1]:
                copy.start()
        if not old:
            form([(s, s, None) for s in range(OWN)], True)
        run_tiles(count)
    if last:
        for out, order in zip(outs, ((0, 1, 2, 3), (4, 5, 8, 9), (10, 11, 6, 7), (12, 13, 14, 15))):
            for k, s in enumerate(order):
                out[k] = acc[s].astype(out.dtype)
    else:
        acc_out[...] = acc[...]


def stage(old, new, z_parts, y_parts, acc=None):
    vmem = pl.BlockSpec(memory_space=pltpu.VMEM)
    hbm = pl.BlockSpec(memory_space=pltpu.HBM)
    last = new == UNITS
    operands = [*z_parts[:new], *y_parts[:new]]
    in_specs = [hbm] * (2 * new)
    if old:
        operands.append(acc)
        in_specs.append(hbm)
    if last:
        out_shape = tuple(
            jax.ShapeDtypeStruct((OWN, COLS, ROWS), kind) for kind in (jnp.float32,) * 4
        )
        out_specs = (vmem,) * 4
    else:
        out_shape = jax.ShapeDtypeStruct((16, COLS, ROWS), jnp.float32)
        out_specs = vmem
    slots = UNIT * new
    return pl.pallas_call(
        functools.partial(stage_kernel, old, new, last),
        out_shape=out_shape,
        in_specs=in_specs,
        out_specs=out_specs,
        scratch_shapes=[
            pltpu.VMEM((new, HALF, FEAT), jnp.bfloat16),
            pltpu.VMEM((new, HALF, FEAT), jnp.bfloat16),
            pltpu.VMEM((slots, COLS, ROWS), jnp.bfloat16),
            pltpu.VMEM((new, SCALED, FEAT), jnp.bfloat16),
            pltpu.VMEM((new, META, FEAT), jnp.bfloat16),
            pltpu.VMEM((new, META, FEAT), jnp.bfloat16),
            pltpu.VMEM((slots, 1, ROWS), jnp.float32),
            pltpu.VMEM((128, ROWS), jnp.float32),
            pltpu.VMEM((slots, ROWS, 128), jnp.float32),
            pltpu.VMEM((2, 16, 128), jnp.int32),
            pltpu.SMEM((16, 128), jnp.int32),
            pltpu.SMEM((16, 128), jnp.int32),
            pltpu.SMEM((2, 16), jnp.int32),
            pltpu.SMEM((264,), jnp.int32),
            pltpu.SMEM((264,), jnp.int32),
            pltpu.VMEM((16, COLS, ROWS), jnp.float32),
            pltpu.SemaphoreType.DMA((new,)),
            pltpu.SemaphoreType.DMA((new,)),
            pltpu.SemaphoreType.DMA((new,)),
            pltpu.SemaphoreType.DMA((new,)),
            pltpu.SemaphoreType.DMA((new,)),
            pltpu.SemaphoreType.DMA((3,)),
        ],
        compiler_params=pltpu.CompilerParams(vmem_limit_bytes=VMEM_LIMIT),
        cost_estimate=pl.CostEstimate(flops=6 * 10**9, bytes_accessed=16 * 2**20, transcendentals=10**6),
        name="stage_%d" % new,
    )(*operands)


def finish_kernel(deg_ref, own_ref, a_ref, b_ref, c_ref, image_ref, gram_ref):
    parts = []
    for b in range(OWN):
        inv = 1.0 / jnp.sqrt(deg_ref[b:b + 1, :])
        far = [ref[b].astype(jnp.float32) for ref in (a_ref, b_ref, c_ref)]
        parts.append((own_ref[b] + far[0] + (far[1] + far[2])) * inv)
    image = jnp.concatenate(parts, axis=1)
    image_ref[...] = image
    gram = lax.dot_general(
        image, image, NT, precision=lax.Precision.HIGHEST, preferred_element_type=jnp.float32
    )
    gram_ref[...] = jnp.concatenate([gram[:COLS // 2], gram[COLS // 2:]], axis=1)


def finish(degree, own, a, b, c):
    return pl.pallas_call(
        finish_kernel,
        out_shape=(
            jax.ShapeDtypeStruct((COLS, DOCS), jnp.float32),
            jax.ShapeDtypeStruct((COLS // 2, 2 * COLS), jnp.float32),
        ),
        compiler_params=pltpu.CompilerParams(vmem_limit_bytes=SMALL_LIMIT),
        name="finish",
    )(degree, own, a, b, c)


def solve_kernel(documents, gram_ref, other_ref, image_hbm, out_ref, image_ref, sem):
    load = pltpu.make_async_copy(image_hbm, image_ref, sem)
    load.start()
    packed = (gram_ref[...] + other_ref[...]) / documents
    gram = jnp.concatenate([packed[:, :COLS], packed[:, COLS:]], axis=0)
    row_id = lax.broadcasted_iota(jnp.int32, (COLS, 2 * COLS), 0)
    lane_id = lax.broadcasted_iota(jnp.int32, (COLS, 2 * COLS), 1)
    unit = (row_id[:, :COLS] == lane_id[:, :COLS]).astype(jnp.float32)
    work = jnp.concatenate([gram, unit], axis=1)
    for start in range(0, COLS, PANEL):
        columns = [jnp.broadcast_to(work[:, start + j:start + j + 1], work.shape) for j in range(PANEL)]
        for j in range(PANEL):
            k = start + j
            factor = columns[j] * (1.0 / columns[j][k:k + 1, :])
            factor = jnp.where(row_id > k, factor, 0.0)
            for i in range(j + 1, PANEL):
                columns[i] = columns[i] - factor * columns[j][start + i:start + i + 1, :]
            work = work - factor * work[k:k + 1, :]
    pivots = jnp.sum(jnp.where(row_id == lane_id, work, 0.0), axis=1, keepdims=True)
    inverse = work[:, COLS:] / jnp.sqrt(pivots)
    load.wait()
    for b in range(OWN):
        out_ref[b] = lax.dot_general(
            inverse, image_ref[:, b * ROWS:(b + 1) * ROWS], NN,
            precision=lax.Precision.HIGHEST, preferred_element_type=jnp.float32,
        )


def solve(documents, gram, other, image):
    vmem = pl.BlockSpec(memory_space=pltpu.VMEM)
    return pl.pallas_call(
        functools.partial(solve_kernel, float(documents)),
        out_shape=jax.ShapeDtypeStruct((OWN, COLS, ROWS), jnp.float32),
        in_specs=[vmem, vmem, pl.BlockSpec(memory_space=pltpu.HBM)],
        scratch_shapes=[pltpu.VMEM((COLS, DOCS), jnp.float32), pltpu.SemaphoreType.DMA],
        compiler_params=pltpu.CompilerParams(vmem_limit_bytes=SMALL_LIMIT),
        name="solve",
    )(gram, other, image)


def shift_z(k):
    return [(y * SIDE + z, y * SIDE + (z + k) % SIDE) for y in range(SIDE) for z in range(SIDE)]


def shift_y(k):
    return [(y * SIDE + z, (y + k) % SIDE * SIDE + z) for y in range(SIDE) for z in range(SIDE)]


def per_device(embedding, subspace, degree, neighbours, counts):
    z_a, z_b, y_a, y_b = prepare(embedding, subspace, degree, neighbours, counts)

    def gather(a, b, shift):
        minus_a = lax.ppermute(a, "blk", shift(1))
        plus_b = lax.ppermute(b, "blk", shift(-1))
        b_next, minus_a = lax.optimization_barrier((b, minus_a))
        a_next, plus_b = lax.optimization_barrier((a, plus_b))
        minus_b = lax.ppermute(b_next, "blk", shift(1))
        plus_a = lax.ppermute(a_next, "blk", shift(-1))
        minus_next, minus_b = lax.optimization_barrier((minus_a, minus_b))
        plus_next, plus_a = lax.optimization_barrier((plus_b, plus_a))
        far_a = lax.ppermute(minus_next, "blk", shift(1))
        far_b = lax.ppermute(plus_next, "blk", shift(-1))
        return a, b, minus_a, plus_b, minus_b, plus_a, far_a, far_b

    z_parts = gather(z_a, z_b, shift_z)
    y_parts = gather(y_a, y_b, shift_y)
    acc = stage(0, 4, z_parts, y_parts)
    acc = stage(4, 6, z_parts, y_parts, acc)
    own, to_minus, to_plus, to_far = stage(6, 8, z_parts, y_parts, acc)
    back_a = lax.ppermute(to_minus, "blk", shift_z(-1))
    back_b = lax.ppermute(to_plus, "blk", shift_z(1))
    back_c = lax.ppermute(to_far, "blk", shift_z(2))
    image, gram = finish(degree, own, back_a, back_b, back_c)

    devices_blk = lax.axis_size("blk")
    devices_dp = lax.axis_size("dp")
    other = lax.ppermute(gram, "dp", [(i, i ^ 1) for i in range(devices_dp)])
    for axis, size, first in (("dp", devices_dp, 2), ("blk", devices_blk, 1)):
        step = first
        while step < size:
            gram = gram + other
            other = lax.ppermute(gram, axis, [(i, i ^ step) for i in range(size)])
            step *= 2
    solved = solve(DOCS * devices_blk * devices_dp, gram, other, image)
    return jnp.swapaxes(solved, 1, 2)


def solution(mesh):
    placed = (
        P(("dp", "blk"), None, None),
        P(("dp", "blk"), None, None),
        P(("dp", "blk"), None),
        P(("dp", "blk"), None),
        P(("dp", "blk")),
    )
    return jax.shard_map(
        per_device,
        mesh=mesh,
        in_specs=placed,
        out_specs=P(("dp", "blk"), None, None),
        check_vma=False,
    )
```
